256 devices in a mesh: rep: 8 (over z), exp: 32 (over x, y, core).
Axes of the slice: x: 4, y: 4, z: 8, core: 2. Of those that a mesh axis runs over, the one named last changes fastest.
Arguments:
- tokens: bfloat16 [8, 4096, 4096], P('rep', 'exp'), may hold values from -6 to 6
- grad_out: bfloat16 [8, 4096, 4096], P('rep', 'exp'), may hold values from -6 to 6
- gates: float32 [8, 2, 128], P('rep'), may hold values from 0.1 to 1
- chosen: int32 [8, 2, 128], P('rep'), may hold values from 0 to 4095, as said below
- w_in: bfloat16 [2, 4096, 8192], P(None, None, 'exp'), may hold values from -0.09375 to 0.09375
- w_out: bfloat16 [2, 8192, 4096], P(None, 'exp'), may hold values from -0.0625 to 0.0625
Outputs:
- d_tokens: bfloat16 [8, 4096, 4096], P('rep', 'exp')
- d_gates: float32 [8, 2, 128], P('rep')
- d_w_in: bfloat16 [2, 4096, 8192], P(None, 'rep', 'exp')
- d_w_out: bfloat16 [2, 8192, 4096], P(None, 'exp', 'rep')
The draws below stay inside these ranges and needn't reach their ends.
Inputs may be any that keep to these rules, and one draw needn't show every extreme that they name: `chosen`: each expert's list in a replica group holds 128 distinct token numbers; at most 8 of them lie among the 128 tokens of one device, and for every expert some device holds exactly 8.
All inputs are finite; a program needn't handle non-finite values.
Results may differ from the reference program's by a relative error of at most 0.02.
Values may be sent and summed in bfloat16 or wider, within the bound.
A program may use at most 192 MiB of HBM per device.

```python
import jax
import jax.numpy as jnp
from jax import lax

D = 4096
FF = 8192
EXPERTS = 2
TOK_DEV = 128
REPS = 8
GROUP_TOK = 4096
CAP = 128
MOST = 8


def draw_chosen(key, part):
    key = jax.random.fold_in(key, 11)
    owner_count = GROUP_TOK // TOK_DEV

    def one_list(sub):
        key_pair, key_split, key_rows, key_order = jax.random.split(sub, 4)
        pairing = jax.random.permutation(key_pair, owner_count)
        split_amount = jax.random.randint(key_split, (owner_count // 2,), 0, MOST + 1)
        split_amount = split_amount.at[0].set(0)
        pair_counts = jnp.stack([split_amount, MOST - split_amount], axis=1).reshape(owner_count)
        counts = jnp.zeros((owner_count,), jnp.int32).at[pairing].set(pair_counts.astype(jnp.int32))
        row_keys = jax.random.split(key_rows, owner_count)
        local_perm = jax.vmap(lambda k: jax.random.permutation(k, TOK_DEV))(row_keys)[:, :MOST]
        owner_ids = jnp.arange(owner_count, dtype=jnp.int32)[:, None] * TOK_DEV + local_perm.astype(jnp.int32)
        valid = jnp.arange(MOST, dtype=jnp.int32)[None, :] < counts[:, None]
        order = jnp.argsort(jnp.where(valid, 0, 1).reshape(-1), stable=True)
        picked = owner_ids.reshape(-1)[order[:CAP]]
        shuffle = jax.random.permutation(key_order, CAP)
        return picked[shuffle].astype(jnp.int32)
    keys = jax.random.split(key, REPS * EXPERTS)
    return jax.vmap(one_list)(keys).reshape(REPS, EXPERTS, CAP)


def shard_levels(stream_key, dims, cuts, smallest, top_value):
    def one(axis_at, blocks):
        draws = jax.random.uniform(jax.random.fold_in(jax.random.fold_in(stream_key, 6), axis_at), (blocks,), jnp.float32, smallest / len(cuts), top_value / len(cuts))
        return jnp.repeat(jnp.exp(draws), dims[axis_at] // blocks).reshape((-1,) + (1,) * (len(dims) - axis_at - 1))

    level = one(*cuts[0])
    for cut in cuts[1:]:
        level = level * one(*cut)
    return level


def noise(rng, shape, spread, reach, pieces=(), kind=jnp.bfloat16):
    drawn = jax.random.normal(rng, shape, jnp.float32) * spread
    if len(pieces) > 0:
        drawn = shard_levels(rng, shape, pieces, -0.22, 0.18) * drawn
    return jnp.clip(drawn, min=-reach, max=reach).astype(kind)


def setup_inputs(seed: int = 0) -> dict:
    key_of = jax.random.split(jax.random.key(seed), 7)
    return {
        "tokens": noise(key_of[0], (REPS, GROUP_TOK, D), 1.0, 6.0, ((0, 8), (1, 32))),
        "grad_out": noise(key_of[1], (REPS, GROUP_TOK, D), 1.0, 6.0, ((0, 8), (1, 32))),
        "gates": jnp.clip(0.1 + 0.9 * jax.random.uniform(key_of[2], (REPS, EXPERTS, CAP), jnp.float32) ** shard_levels(key_of[2], (REPS, EXPERTS, CAP), ((0, 8),), -0.2, 0.2), 0.1, 1.0),
        "chosen": draw_chosen(jax.random.fold_in(key_of[6], 71), 0),
        "w_in": noise(key_of[4], (EXPERTS, D, FF), D ** -0.5, 0.09375, ((2, 32),)),
        "w_out": noise(key_of[5], (EXPERTS, FF, D), FF ** -0.5, 0.0625, ((1, 32),)),
    }


GELU_SCALE = 0.7978845608028654
GELU_CUBIC = 0.044715


def gelu_parts(hidden):
    tangent = jnp.tanh(GELU_SCALE * (hidden + GELU_CUBIC * hidden * hidden * hidden))
    activated = 0.5 * hidden * (1.0 + tangent)
    slope = 0.5 * (1.0 + tangent) + 0.5 * hidden * (1.0 - tangent * tangent) * GELU_SCALE * (1.0 + 3.0 * GELU_CUBIC * hidden * hidden)
    return activated, slope


def reference(tokens, grad_out, gates, chosen, w_in, w_out):
    def one_group(totals, items):
        total_in, total_out = totals
        tok_group, grad_group, gate_group, chosen_group = items
        d_tok = jnp.zeros((GROUP_TOK, D), jnp.float32)
        gate_list = []
        for expert in range(EXPERTS):
            index_row = chosen_group[expert].astype(jnp.int32)
            rows = jnp.take(tok_group, index_row, axis=0)
            grad_rows = jnp.take(grad_group, index_row, axis=0)
            gate_col = gate_group[expert][:, None]
            hidden = jnp.dot(rows, w_in[expert], preferred_element_type=jnp.float32)
            activated, slope = gelu_parts(hidden)
            activated = activated.astype(jnp.bfloat16)
            back_proj = jnp.dot(grad_rows, w_out[expert].T, preferred_element_type=jnp.float32)
            gate_list.append(jnp.sum(activated.astype(jnp.float32) * back_proj, axis=1))
            scaled = (gate_col * grad_rows.astype(jnp.float32)).astype(jnp.bfloat16)
            d_hidden = (gate_col * back_proj * slope).astype(jnp.bfloat16)
            slot_grad = jnp.dot(d_hidden, w_in[expert].T, preferred_element_type=jnp.float32)
            d_tok = d_tok.at[index_row].add(slot_grad)
            part_in = jnp.dot(rows.T, d_hidden, preferred_element_type=jnp.float32)
            part_out = jnp.dot(activated.T, scaled, preferred_element_type=jnp.float32)
            part_in = lax.optimization_barrier(part_in.astype(jnp.bfloat16)).astype(jnp.float32)
            part_out = lax.optimization_barrier(part_out.astype(jnp.bfloat16)).astype(jnp.float32)
            total_in = total_in.at[expert].add(part_in)
            total_out = total_out.at[expert].add(part_out)
        return (total_in, total_out), (d_tok.astype(jnp.bfloat16), jnp.stack(gate_list))

    start_in = jnp.zeros((EXPERTS, D, FF), jnp.float32)
    start_out = jnp.zeros((EXPERTS, FF, D), jnp.float32)
    (total_in, total_out), (d_tokens, d_gates) = lax.scan(one_group, (start_in, start_out), (tokens, grad_out, gates, chosen))
    return d_tokens, d_gates, total_in.astype(jnp.bfloat16), total_out.astype(jnp.bfloat16)
```

```python
import functools

import jax
import jax.numpy as jnp
from jax import lax
from jax.experimental import pallas as pl
from jax.experimental.pallas import tpu as pltpu
from jax.sharding import PartitionSpec as P

GELU_SCALE = 0.7978845608028654
GELU_CUBIC = 0.044715

BF = jnp.bfloat16
F32 = jnp.float32
MESH = pl.DeviceIdType.MESH

NX, NY, NZ = 4, 4, 8
D = 4096
F = 256
CAP = 128
TOK = 128
MOST = 8
ROWS = 2 * MOST
PAD = NX * NY * 2 * ROWS
HALF = D // 2
DS_W = D // NZ
BLK = 512

NSEM = 96


def dot(a, b, ca=1, cb=0):
    return lax.dot_general(a, b, (((ca,), (cb,)), ((), ())), preferred_element_type=F32)


def kernel(
    tok_hbm, grad_hbm, gates_ref, chosen_ref, win_hbm, wout_hbm,
    dtok_ref, dgate_ref, dwin_ref, dwout_ref,
    tok, grad, win, wout, xg, dg, cc, ds, zb, acc, ps, rsib, rs1, ts, rs2, gbuf, gsib, gx, gy,
    ssem, rsem, lsem,
):
    r = lax.axis_index("rep")
    e = lax.axis_index("exp")
    x = e // 8
    y = (e // 2) % 4
    c = e % 2
    oc = 1 - c

    def dev(rr, xx, yy, c_):
        return (rr, (xx * 4 + yy) * 2 + c_)

    def xs(d):
        return lax.rem(x + d, 4)

    def ys(d):
        return lax.rem(y + d, 4)

    def zs(d):
        return lax.rem(r + d, 8)

    sib = dev(r, x, y, oc)

    loads = [
        pltpu.make_async_copy(tok_hbm.at[0], tok, lsem.at[0]),
        pltpu.make_async_copy(grad_hbm.at[0], grad, lsem.at[1]),
        pltpu.make_async_copy(win_hbm, win, lsem.at[2]),
        pltpu.make_async_copy(wout_hbm, wout, lsem.at[3]),
    ]
    for load in loads:
        load.start()

    barrier = pltpu.get_barrier_semaphore()
    partners = (
        [sib]
        + [dev(r, xs(d), y, c) for d in (1, 2, 3)]
        + [dev(r, x, ys(d), c) for d in (1, 2, 3)]
        + [dev(zs(d), x, y, c) for d in range(1, 8)]
    )
    for p in partners:
        pl.semaphore_signal(barrier, inc=1, device_id=p, device_id_type=MESH)

    counter = [0]
    sent = []

    def send(src, dst, to):
        i = counter[0]
        counter[0] += 1
        cp = pltpu.make_async_remote_copy(
            src_ref=src, dst_ref=dst, send_sem=ssem.at[i], recv_sem=rsem.at[i],
            device_id=to, device_id_type=MESH,
        )
        cp.start()
        sent.append(cp)
        return cp

    def iota(shape, dim):
        return lax.broadcasted_iota(jnp.int32, shape, dim)

    sq = (CAP, CAP)
    ch_row, ch_col, pos_row, pos_col, gate_col = [], [], [], [], []
    for k in range(2):
        row = chosen_ref[0, k : k + 1, :]
        rb = jnp.broadcast_to(row, sq)
        cb = rb.T
        ob_row, ob_col = rb // TOK, cb // TOK
        same = (ob_row == ob_col)
        before_row = jnp.where(same & (iota(sq, 1) < iota(sq, 0)), 1, 0)
        before_col = jnp.where(same & (iota(sq, 0) < iota(sq, 1)), 1, 0)
        rank_col = jnp.sum(before_row, axis=1, keepdims=True)
        rank_row = jnp.sum(before_col, axis=0, keepdims=True)

        def place(own, rank):
            return ((own % 2) * (NX * NY) + own // 2) * ROWS + k * MOST + rank

        ch_row.append(row)
        ch_col.append(cb[:, 0:1])
        pos_row.append(place(row // TOK, rank_row))
        pos_col.append(place(cb[:, 0:1] // TOK, rank_col))
        gate_col.append(jnp.broadcast_to(gates_ref[0, k : k + 1, :], sq).T[:, 0:1])

    my_first = (c * (NX * NY) + x * NY + y) * ROWS

    def hot(m):
        return jnp.where(m, 1.0, 0.0).astype(BF)

    pick = jnp.zeros((ROWS, TOK), F32)
    unpick = jnp.zeros((TOK, 2 * ROWS), F32)
    for k in range(2):
        a = hot(pos_row[k] - my_first == iota((ROWS, CAP), 0))
        b = hot(ch_col[k] - e * TOK == iota((CAP, TOK), 1))
        pick += dot(a, b)
        bt = hot(ch_row[k] - e * TOK == iota((TOK, CAP), 0))
        at = hot(pos_col[k] - my_first == iota((CAP, 2 * ROWS), 1) % ROWS)
        unpick += dot(bt, at)
    pick = pick.astype(BF)
    unpick = unpick.astype(BF)
    expand = [hot(pos_row[k] == iota((PAD, CAP), 0)) for k in range(2)]
    gather = jnp.concatenate([hot(pos_col[k] == iota((CAP, PAD), 1)) for k in range(2)], axis=0)

    loads[0].wait()
    loads[1].wait()

    @pl.loop(0, D // BLK)
    def _(j):
        cols = pl.ds(pl.multiple_of(j * BLK, BLK), BLK)
        xg[c, x, y, :, cols] = dot(pick, tok[:, cols]).astype(BF)
        dg[c, x, y, :, cols] = dot(pick, grad[:, cols]).astype(BF)

    pl.semaphore_wait(barrier, len(partners))

    p1 = []
    for d in (1, 3, 2):
        p1.append(send(xg.at[c, x, y], xg.at[c, x, y], dev(r, xs(d), y, c)))
        p1.append(send(dg.at[c, x, y], dg.at[c, x, y], dev(r, x, ys(d), c)))
    for cp in p1:
        cp.wait_recv()
    up_x = send(xg.at[c, :, y], xg.at[c, :, y], dev(r, x, ys(1), c))
    up_d = send(dg.at[c, x], dg.at[c, x], dev(r, xs(1), y, c))
    dn_x = send(xg.at[c, :, y], xg.at[c, :, y], dev(r, x, ys(3), c))
    dn_d = send(dg.at[c, x], dg.at[c, x], dev(r, xs(3), y, c))
    sibs = [send(xg.at[c, :, y], xg.at[c, :, y], sib), send(dg.at[c, x], dg.at[c, x], sib)]
    loads[2].wait()
    loads[3].wait()
    up_x.wait_recv()
    fw = [send(xg.at[c, 0:2, ys(3)], xg.at[c, 0:2, ys(3)], dev(r, x, ys(1), c))]
    up_d.wait_recv()
    fw.append(send(dg.at[c, xs(3), 0:2], dg.at[c, xs(3), 0:2], dev(r, xs(1), y, c)))
    dn_x.wait_recv()
    fw.append(send(xg.at[c, 2:4, ys(1)], xg.at[c, 2:4, ys(1)], dev(r, x, ys(3), c)))
    dn_d.wait_recv()
    fw.append(send(dg.at[c, xs(1), 2:4], dg.at[c, xs(1), 2:4], dev(r, xs(3), y, c)))
    for d in (1, 3):
        sibs.append(send(xg.at[c, :, ys(d)], xg.at[c, :, ys(d)], sib))
        sibs.append(send(dg.at[c, xs(d)], dg.at[c, xs(d)], sib))
    for cp in fw:
        cp.wait_recv()
    sibs.append(send(xg.at[c, :, ys(2)], xg.at[c, :, ys(2)], sib))
    sibs.append(send(dg.at[c, xs(2)], dg.at[c, xs(2)], sib))
    for cp in sibs:
        cp.wait_recv()

    acc[...] = jnp.zeros_like(acc)
    gcol = jnp.concatenate(gate_col, axis=0)

    @pl.loop(0, D // BLK)
    def _(j):
        cols = pl.ds(pl.multiple_of(j * BLK, BLK), BLK)
        xc = dot(gather, xg[:, :, :, :, cols].reshape(PAD, BLK)).astype(BF)
        dc = dot(gather, dg[:, :, :, :, cols].reshape(PAD, BLK))
        cc[0, :, :, cols] = xc.reshape(NX * NY, ROWS, BLK)
        cc[1, :, :, cols] = (gcol * dc).astype(BF).reshape(NX * NY, ROWS, BLK)
        dc = dc.astype(BF)
        for k in range(2):
            sl = slice(k * CAP, (k + 1) * CAP)
            acc[0, k] += dot(xc[sl], win[k, cols, :])
            acc[1, k] += dot(dc[sl], wout[k, :, cols], 1, 1)

    dpad = []
    for k in range(2):
        hidden = acc[0, k]
        back = acc[1, k]
        tang = jnp.tanh(GELU_SCALE * (hidden + GELU_CUBIC * hidden * hidden * hidden))
        act = (0.5 * hidden * (1.0 + tang)).astype(BF)
        slope = 0.5 * (1.0 + tang) + 0.5 * hidden * (1.0 - tang * tang) * GELU_SCALE * (
            1.0 + 3.0 * GELU_CUBIC * hidden * hidden
        )
        dh = (gate_col[k] * back * slope).astype(BF)
        zb[r, 0, k] = act
        zb[r, 1, k] = dh
        gbuf[0, k] = lax.dot_general(
            jnp.ones((8, F), F32), act.astype(F32) * back, (((1,), (1,)), ((), ())),
            precision=lax.Precision.HIGHEST, preferred_element_type=F32,
        )
        dpad.append(dot(expand[k], dh).astype(BF))

    right, left = dev(zs(1), x, y, c), dev(zs(7), x, y, c)
    zr = send(zb.at[r], zb.at[r], right)
    zl = send(zb.at[r], zb.at[r], left)

    chip = x * NY + y
    own_ds = pltpu.make_async_copy(
        cc.at[c, chip, :, pl.ds(pl.multiple_of(r * DS_W, DS_W), DS_W)], ds.at[c, r, x, y], lsem.at[0]
    )
    own_ds.start()
    ex = []
    for d in (1, 7, 2, 6, 3, 5, 4):
        cols = pl.ds(pl.multiple_of(zs(d) * DS_W, DS_W), DS_W)
        ex.append(send(cc.at[c, chip, :, cols], ds.at[c, r, x, y], dev(zs(d), x, y, c)))
    g0 = send(gbuf.at[0], gsib, sib)

    halves = []
    for h in range(2):

        @pl.loop(h * (HALF // BLK), (h + 1) * (HALF // BLK))
        def _(j):
            cols = pl.ds(pl.multiple_of(j * BLK, BLK), BLK)
            part = dot(dpad[0], win[0, cols, :], 1, 1) + dot(dpad[1], win[1, cols, :], 1, 1)
            ps[:, :, :, :, cols] = part.astype(BF).reshape(2, NX, NY, ROWS, BLK)

        hc = pl.ds(h * HALF, HALF)
        halves.append(send(ps.at[oc, :, :, :, hc], rsib.at[:, :, :, hc], sib))

    own_ds.wait()
    for cp in ex:
        cp.wait_recv()
    q1 = []
    for d in (1, 3, 2):
        q1.append(send(ds.at[c, 0:4, x, y], ds.at[c, 0:4, x, y], dev(r, xs(d), y, c)))
        q1.append(send(ds.at[c, 4:8, x, y], ds.at[c, 4:8, x, y], dev(r, x, ys(d), c)))

    g0.wait_recv()
    gbuf[1] = gbuf[0] + gsib[...]
    gx[x] = gbuf[1]
    g1 = [send(gbuf.at[1], gx.at[x], dev(r, xs(d), y, c)) for d in (1, 3, 2)]

    zr.wait_recv()
    zr = send(zb.at[zs(7)], zb.at[zs(7)], right)
    zl.wait_recv()
    zl = send(zb.at[zs(1)], zb.at[zs(1)], left)

    stage1 = []
    for h in range(2):
        halves[h].wait_recv()
        hc = pl.ds(h * HALF, HALF)

        @pl.loop(0, NX)
        def _(i):
            for j in range(NY):
                own = ps[c, i, j, :, hc].astype(F32)
                ps[c, i, j, :, hc] = (own + rsib[i, j, :, hc].astype(F32)).astype(BF)

        for d in (1, 3, 2):
            if h == 0:
                stage1.append(send(ps.at[c, xs(d), :, :, hc], rs1.at[0, x], dev(r, xs(d), y, c)))
            else:
                stage1.append(send(ps.at[c, :, ys(d), :, hc], rs1.at[1, y], dev(r, x, ys(d), c)))

    for cp in q1:
        cp.wait_recv()
    q2 = []
    for d in (1, 3, 2):
        q2.append(send(ds.at[c, 0:4, :, y], ds.at[c, 0:4, :, y], dev(r, x, ys(d), c)))
        q2.append(send(ds.at[c, 4:8, x], ds.at[c, 4:8, x], dev(r, xs(d), y, c)))

    zr.wait_recv()
    zr = send(zb.at[zs(6)], zb.at[zs(6)], right)
    zl.wait_recv()
    zl = send(zb.at[zs(2)], zb.at[zs(2)], left)

    for cp in g1:
        cp.wait_recv()
    gbuf[2] = (gx[0] + gx[1]) + (gx[2] + gx[3])
    gy[y] = gbuf[2]
    g2 = [send(gbuf.at[2], gy.at[y], dev(r, x, ys(d), c)) for d in (1, 3, 2)]

    stage2 = []
    for h in range(2):
        for cp in stage1[3 * h : 3 * h + 3]:
            cp.wait_recv()
        hc = pl.ds(h * HALF, HALF)
        for j in range(4):
            total = (ps[c, x, j, :, hc] if h == 0 else ps[c, j, y, :, hc]).astype(F32)
            for d in (1, 2, 3):
                total += rs1[h, xs(d) if h == 0 else ys(d), j].astype(F32)
            ts[h, j] = total.astype(BF)
        for d in (1, 3, 2):
            if h == 0:
                stage2.append(send(ts.at[0, ys(d)], rs2.at[0, y], dev(r, x, ys(d), c)))
            else:
                stage2.append(send(ts.at[1, xs(d)], rs2.at[1, x], dev(r, xs(d), y, c)))

    zr.wait_recv()
    zr = send(zb.at[zs(5), 0], zb.at[zs(5), 0], right)
    zl.wait_recv()
    zl = send(zb.at[zs(3), 1], zb.at[zs(3), 1], left)

    for cp in q2:
        cp.wait_recv()
    q3 = send(ds.at[c], ds.at[c], sib)

    for cp in g2:
        cp.wait_recv()
    total = (gy[0] + gy[1]) + (gy[2] + gy[3])
    for k in range(2):
        dgate_ref[0, k : k + 1, :] = total[k, 0:1, :]

    for h in range(2):
        for cp in stage2[3 * h : 3 * h + 3]:
            cp.wait_recv()
        total = ts[h, y if h == 0 else x].astype(F32)
        for d in (1, 2, 3):
            total += rs2[h, ys(d) if h == 0 else xs(d)].astype(F32)
        high = total.astype(BF)
        low = (total - high.astype(F32)).astype(BF)
        both = jnp.concatenate([high, low], axis=0)
        for j in range(HALF // BLK):
            dtok_ref[0, :, h * HALF + j * BLK : h * HALF + (j + 1) * BLK] = dot(
                unpick, both[:, j * BLK : (j + 1) * BLK]
            ).astype(BF)

    zr.wait_recv()
    zl.wait_recv()
    q3.wait_recv()
    for k in range(2):
        xk = ds[0, :, 2 * k : 2 * k + 2].reshape(NZ * CAP, DS_W)
        sk = ds[1, :, 2 * k : 2 * k + 2].reshape(NZ * CAP, DS_W)
        dwin_ref[k] = dot(xk, zb[:, 1, k].reshape(NZ * CAP, F), 0, 0).astype(BF)
        dwout_ref[k] = dot(zb[:, 0, k].reshape(NZ * CAP, F), sk, 0, 0).astype(BF)

    assert counter[0] <= NSEM, counter[0]
    for cp in sent:
        cp.wait_send()


def local(tokens, grad_out, gates, chosen, w_in, w_out):
    hbm = pl.BlockSpec(memory_space=pl.ANY)
    vmem = pl.BlockSpec(memory_space=pltpu.VMEM)
    return pl.pallas_call(
        kernel,
        out_shape=(
            jax.ShapeDtypeStruct((1, TOK, D), BF),
            jax.ShapeDtypeStruct((1, 2, CAP), F32),
            jax.ShapeDtypeStruct((2, DS_W, F), BF),
            jax.ShapeDtypeStruct((2, F, DS_W), BF),
        ),
        in_specs=[hbm, hbm, vmem, vmem, hbm, hbm],
        out_specs=(vmem, vmem, vmem, vmem),
        scratch_shapes=[
            pltpu.VMEM((TOK, D), BF),
            pltpu.VMEM((TOK, D), BF),
            pltpu.VMEM((2, D, F), BF),
            pltpu.VMEM((2, F, D), BF),
            pltpu.VMEM((2, NX, NY, ROWS, D), BF),
            pltpu.VMEM((2, NX, NY, ROWS, D), BF),
            pltpu.VMEM((2, NX * NY, ROWS, D), BF),
            pltpu.VMEM((2, NZ, NX, NY, ROWS, DS_W), BF),
            pltpu.VMEM((NZ, 2, 2, CAP, F), BF),
            pltpu.VMEM((2, 2, CAP, F), F32),
            pltpu.VMEM((2, NX, NY, ROWS, D), BF),
            pltpu.VMEM((NX, NY, ROWS, D), BF),
            pltpu.VMEM((2, 4, 4, ROWS, HALF), BF),
            pltpu.VMEM((2, 4, ROWS, HALF), BF),
            pltpu.VMEM((2, 4, ROWS, HALF), BF),
            pltpu.VMEM((3, 2, 8, CAP), F32),
            pltpu.VMEM((2, 8, CAP), F32),
            pltpu.VMEM((4, 2, 8, CAP), F32),
            pltpu.VMEM((4, 2, 8, CAP), F32),
            pltpu.SemaphoreType.DMA((NSEM,)),
            pltpu.SemaphoreType.DMA((NSEM,)),
            pltpu.SemaphoreType.DMA((4,)),
        ],
        compiler_params=pltpu.CompilerParams(
            collective_id=0, has_side_effects=True, vmem_limit_bytes=60 << 20
        ),
        name="expert_backward",
    )(tokens, grad_out, gates, chosen, w_in, w_out)


def solution(mesh):
    return jax.shard_map(
        local,
        mesh=mesh,
        in_specs=(
            P("rep", "exp", None),
            P("rep", "exp", None),
            P("rep", None, None),
            P("rep", None, None),
            P(None, None, "exp"),
            P(None, "exp", None),
        ),
        out_specs=(
            P("rep", "exp", None),
            P("rep", None, None),
            P(None, "rep", "exp"),
            P(None, "exp", "rep"),
        ),
        check_vma=False,
    )
```

```python
import jax
import jax.numpy as jnp
from jax import lax
from jax.experimental import pallas as pl
from jax.experimental.pallas import tpu as pltpu
from jax.sharding import PartitionSpec as P

GELU_SCALE = 0.7978845608028654
GELU_CUBIC = 0.044715

BF = jnp.bfloat16
F32 = jnp.float32
MESH = pl.DeviceIdType.MESH

NX, NY, NZ = 4, 4, 8
D = 4096
F = 256
CAP = 128
TOK = 128
MOST = 8
ROWS = 2 * MOST
PAD = NX * NY * 2 * ROWS
COL = 128
BLK = D // NX
PLANE = NX * NY * 2

NSEM = 104


def dot(a, b, ca=1, cb=0):
    return lax.dot_general(a, b, (((ca,), (cb,)), ((), ())), preferred_element_type=F32)


def kernel(
    tok_hbm, grad_hbm, gates_ref, chosen_ref, win_hbm, wout_hbm,
    rows_ref, unpick_ref, dgate_ref, dwin_ref, dwout_ref,
    tok, grad, win, wout, pk, rp, xc, gc, eb, ds, zb, acc, ps, rsib, rs1, ts, rs2, ob, rb,
    gbuf, gsib, gx, gy,
    ssem, rsem, asem, arsem, bsem, brsem, lsem,
):
    r = lax.axis_index("rep")
    e = lax.axis_index("exp")
    x = e // 8
    y = (e // 2) % 4
    c = e % 2
    oc = 1 - c
    chip = x * NY + y

    def dev(rr, xx, yy, c_):
        return (rr, (xx * 4 + yy) * 2 + c_)

    def xs(d):
        return lax.rem(x + d, 4)

    def ys(d):
        return lax.rem(y + d, 4)

    def zs(d):
        return lax.rem(r + d, 8)

    sib = dev(r, x, y, oc)

    loads = [
        pltpu.make_async_copy(tok_hbm.at[0], tok, lsem.at[0]),
        pltpu.make_async_copy(grad_hbm.at[0], grad, lsem.at[1]),
        pltpu.make_async_copy(win_hbm, win, lsem.at[2]),
        pltpu.make_async_copy(wout_hbm, wout, lsem.at[3]),
    ]
    loads[0].start()
    loads[1].start()

    def partner(i):
        return lax.rem(x + i // 8, 4), lax.rem(y + (i // 2) % 4, 4), lax.rem(c + i, 2)

    barrier = pltpu.get_barrier_semaphore()

    @pl.loop(1, PLANE)
    def _(i):
        px, py, pc = partner(i)
        pl.semaphore_signal(barrier, inc=1, device_id=dev(r, px, py, pc), device_id_type=MESH)

    for d in range(1, NZ):
        pl.semaphore_signal(barrier, inc=1, device_id=dev(zs(d), x, y, c), device_id_type=MESH)

    counter = [0]
    sent = []

    def send(src, dst, to):
        i = counter[0]
        counter[0] += 1
        cp = pltpu.make_async_remote_copy(
            src_ref=src, dst_ref=dst, send_sem=ssem.at[i], recv_sem=rsem.at[i],
            device_id=to, device_id_type=MESH,
        )
        cp.start()
        sent.append(cp)
        return cp

    def iota(shape, dim):
        return lax.broadcasted_iota(jnp.int32, shape, dim)

    def hot(m):
        return jnp.where(m, 1.0, 0.0).astype(BF)

    sq = (CAP, CAP)
    my_first = (c * (NX * NY) + chip) * ROWS
    ch_row, ch_col, pos_row, pos_col, gate_col = [], [], [], [], []
    for k in range(2):
        row = chosen_ref[0, k : k + 1, :]
        rb_ = jnp.broadcast_to(row, sq)
        cb_ = rb_.T
        same = (rb_ // TOK) == (cb_ // TOK)
        rank_col = jnp.sum(jnp.where(same & (iota(sq, 1) < iota(sq, 0)), 1, 0), axis=1, keepdims=True)
        rank_row = jnp.sum(jnp.where(same & (iota(sq, 0) < iota(sq, 1)), 1, 0), axis=0, keepdims=True)

        def place(own, rank):
            return ((own % 2) * (NX * NY) + own // 2) * ROWS + k * MOST + rank

        ch_row.append(row)
        ch_col.append(cb_[:, 0:1])
        pos_row.append(place(row // TOK, rank_row))
        pos_col.append(place(cb_[:, 0:1] // TOK, rank_col))

    pick = jnp.zeros((ROWS, TOK), F32)
    for k in range(2):
        a = hot(pos_row[k] - my_first == iota((ROWS, CAP), 0))
        b = hot(ch_col[k] - e * TOK == iota((CAP, TOK), 1))
        pick += dot(a, b)
    pick = pick.astype(BF)

    loads[0].wait()
    loads[1].wait()
    loads[2].start()
    loads[3].start()

    @pl.loop(0, NX)
    def _(i):
        cols = pl.ds(pl.multiple_of(i * BLK, BLK), BLK)
        xr = dot(pick, tok[:, cols]).astype(BF)
        dr = dot(pick, grad[:, cols]).astype(BF)
        for j in range(NY):
            for k in range(2):
                at = slice((2 * j + k) * COL, (2 * j + k + 1) * COL)
                pk[k, i, j, 0] = xr[:, at]
                pk[k, i, j, 1] = dr[:, at]

    pl.semaphore_wait(barrier, PLANE - 1 + NZ - 1)

    def forth(i):
        px, py, pc = partner(i)
        return pltpu.make_async_remote_copy(
            src_ref=pk.at[pc, px, py], dst_ref=rp.at[c, x, y], send_sem=asem.at[i],
            recv_sem=arsem.at[i], device_id=dev(r, px, py, pc), device_id_type=MESH,
        )

    @pl.loop(1, PLANE)
    def _(i):
        forth(i).start()

    rp[c, x, y] = pk[c, x, y]
    gather = jnp.concatenate([hot(pos_col[k] == iota((CAP, PAD), 1)) for k in range(2)], axis=0)
    for k in range(2):
        gate_col.append(jnp.broadcast_to(gates_ref[0, k : k + 1, :], sq).T)
        gc[k * 8 : (k + 1) * 8] = gate_col[k].reshape(8, ROWS, COL)

    @pl.loop(1, PLANE)
    def _(i):
        forth(i).wait_recv()

    both = jnp.concatenate([rp[:, :, :, k].reshape(PAD, COL) for k in range(2)], axis=1)
    both = dot(gather, both).astype(BF)
    for a in range(2):
        for k in range(2):
            xc[a, k, c, x, y] = both[k * CAP : (k + 1) * CAP, a * COL : (a + 1) * COL]

    p1 = [[], []]
    for a in range(2):
        for d in (1, 3, 2):
            for k, to in ((0, dev(r, xs(d), y, c)), (1, dev(r, x, ys(d), c))):
                p1[a].append(send(xc.at[a, k, c, x, y], xc.at[a, k, c, x, y], to))

    def row(a, k, d):
        return xc.at[a, 0, c, :, ys(d)] if k == 0 else xc.at[a, 1, c, xs(d)]

    def half(a, k, d, h):
        return xc.at[a, 0, c, 2 * h : 2 * h + 2, ys(d)] if k == 0 else xc.at[a, 1, c, xs(d), 2 * h : 2 * h + 2]

    def along(k, d):
        return dev(r, x, ys(d), c) if k == 0 else dev(r, xs(d), y, c)

    p2, fw, sibs = [[], []], [[], []], [[], []]
    for a in range(2):
        for cp in p1[a]:
            cp.wait_recv()
        for k in range(2):
            p2[a].append(send(row(a, k, 0), row(a, k, 0), along(k, 1)))
            p2[a].append(send(row(a, k, 0), row(a, k, 0), along(k, 3)))
        for k in range(2):
            sibs[a].append(send(row(a, k, 0), row(a, k, 0), sib))
    loads[2].wait()
    loads[3].wait()
    for a in range(2):
        for k in range(2):
            p2[a][2 * k].wait_recv()
            fw[a].append(send(half(a, k, 3, 0), half(a, k, 3, 0), along(k, 1)))
            p2[a][2 * k + 1].wait_recv()
            fw[a].append(send(half(a, k, 1, 1), half(a, k, 1, 1), along(k, 3)))
        for k in range(2):
            for d in (3, 1):
                sibs[a].append(send(row(a, k, d), row(a, k, d), sib))

    right, left = dev(zs(1), x, y, c), dev(zs(7), x, y, c)
    ring = [None, None]

    def zstep(w, s):
        if s > 1:
            for cp in ring[w]:
                cp.wait_recv()
        if s < 4:
            ra, la = zb.at[w, zs(9 - s)], zb.at[w, zs(s - 1)]
        elif s == 4:
            ra, la = zb.at[w, zs(5), 0], zb.at[w, zs(3), 1]
        else:
            return
        ring[w] = [send(ra, ra, right), send(la, la, left)]

    acc[...] = jnp.zeros_like(acc)
    acts, dhs, backs = [], [], []
    for a in range(2):
        for cp in fw[a]:
            cp.wait_recv()
        for k in range(2):
            sibs[a].append(send(row(a, k, 2), row(a, k, 2), sib))
        for cp in sibs[a]:
            cp.wait_recv()

        @pl.loop(0, NX)
        def _(i):
            cols = pl.ds(pl.multiple_of(i * BLK, BLK), BLK)
            for k in range(2):
                lhs = jnp.concatenate(
                    [xc[a, k, h, i, j] for j in range(NY) for h in range(2)], axis=1
                )
                if a == 0:
                    acc[0, k] += dot(lhs, win[k, cols, :])
                else:
                    acc[1, k] += dot(lhs, wout[k, :, cols], 1, 1)

        if a == 0:
            slopes = []
            for k in range(2):
                hidden = acc[0, k]
                tang = jnp.tanh(GELU_SCALE * (hidden + GELU_CUBIC * hidden * hidden * hidden))
                acts.append((0.5 * hidden * (1.0 + tang)).astype(BF))
                slope = 0.5 * (1.0 + tang) + 0.5 * hidden * (1.0 - tang * tang) * GELU_SCALE * (
                    1.0 + 3.0 * GELU_CUBIC * hidden * hidden
                )
                acc[0, k] = slope
                zb[0, r, k] = acts[k]
            zstep(0, 1)
    for k in range(2):
        dhs.append((gate_col[k][:, 0:1] * acc[1, k] * acc[0, k]).astype(BF))
        zb[1, r, k] = dhs[k]
    zstep(1, 1)
    zstep(0, 2)
    for k in range(2):
        gbuf[0, k] = lax.dot_general(
            jnp.ones((8, F), F32), zb[0, r, k].astype(F32) * acc[1, k], (((1,), (1,)), ((), ())),
            precision=lax.Precision.HIGHEST, preferred_element_type=F32,
        )
    g0 = send(gbuf.at[0], gsib, sib)

    factor = jnp.where(c == 0, 1.0, gc[chip])
    slots = pl.ds(pl.multiple_of(lax.rem(chip, 8) * ROWS, ROWS), ROWS)

    @pl.loop(0, NX)
    def _(i):
        for j in range(NY):
            for h in range(2):
                eb[i, j, h] = (factor * xc[c, x // 2, h, i, j, slots, :].astype(F32)).astype(BF)

    ex = []
    for d in (1, 7, 2, 6, 3, 5, 4):
        to = zs(d)
        ex.append(send(eb.at[to // 2, pl.ds(2 * lax.rem(to, 2), 2)], ds.at[c, x, y, r], dev(to, x, y, c)))
    ds[c, x, y, r] = eb[r // 2, pl.ds(2 * lax.rem(r, 2), 2)]

    pair = []
    for k in range(2):

        @pl.loop(0, NX)
        def _(i):
            cols = pl.ds(pl.multiple_of(i * BLK, BLK), BLK)
            part = dot(zb[1, r, k], win[k, cols, :], 1, 1).astype(BF)
            for j in range(NY):
                for h in range(2):
                    ps[k, h, i, j] = part[:, (2 * j + h) * COL : (2 * j + h + 1) * COL]

        pair.append(send(ps.at[k, oc], rsib.at[k], sib))

    for cp in ex:
        cp.wait_recv()
    q1 = []
    for d in (1, 3, 2):
        q1.append(send(ds.at[c, x, y, 0:4], ds.at[c, x, y, 0:4], dev(r, xs(d), y, c)))
        q1.append(send(ds.at[c, x, y, 4:8], ds.at[c, x, y, 4:8], dev(r, x, ys(d), c)))

    zstep(1, 2)

    stage1 = [[], []]
    for k in range(2):
        pair[k].wait_recv()

        @pl.loop(0, NX)
        def _(i):
            for j in range(NY):
                ps[k, c, i, j] = (ps[k, c, i, j].astype(F32) + rsib[k, i, j].astype(F32)).astype(BF)

        for d in (1, 3, 2):
            if k == 0:
                stage1[k].append(send(ps.at[0, c, xs(d)], rs1.at[0, x], dev(r, xs(d), y, c)))
            else:
                stage1[k].append(send(ps.at[1, c, :, ys(d)], rs1.at[1, y], dev(r, x, ys(d), c)))

    zstep(0, 3)

    g0.wait_recv()
    gbuf[1] = gbuf[0] + gsib[...]
    gx[x] = gbuf[1]
    g1 = [send(gbuf.at[1], gx.at[x], dev(r, xs(d), y, c)) for d in (1, 3, 2)]

    for cp in q1:
        cp.wait_recv()
    q2 = []
    for d in (1, 3, 2):
        q2.append(send(ds.at[c, :, y, 0:4], ds.at[c, :, y, 0:4], dev(r, x, ys(d), c)))
        q2.append(send(ds.at[c, x, :, 4:8], ds.at[c, x, :, 4:8], dev(r, xs(d), y, c)))
    zstep(1, 3)

    stage2 = [[], []]
    for k in range(2):
        for cp in stage1[k]:
            cp.wait_recv()
        for j in range(4):
            total = (ps[0, c, x, j] if k == 0 else ps[1, c, j, y]).astype(F32)
            for d in (1, 2, 3):
                total += rs1[k, xs(d) if k == 0 else ys(d), j].astype(F32)
            ts[k, j] = total.astype(BF)
        for d in (1, 3, 2):
            if k == 0:
                stage2[k].append(send(ts.at[0, ys(d)], rs2.at[0, y], dev(r, x, ys(d), c)))
            else:
                stage2[k].append(send(ts.at[1, xs(d)], rs2.at[1, x], dev(r, xs(d), y, c)))

    zstep(0, 4)
    for cp in g1:
        cp.wait_recv()
    gbuf[2] = (gx[0] + gx[1]) + (gx[2] + gx[3])
    gy[y] = gbuf[2]
    g2 = [send(gbuf.at[2], gy.at[y], dev(r, x, ys(d), c)) for d in (1, 3, 2)]

    expand = jnp.concatenate([hot(pos_row[k] == iota((PAD, CAP), 0)) for k in range(2)], axis=1)
    sums = []
    for k in range(2):
        for cp in stage2[k]:
            cp.wait_recv()
        total = ts[k, y if k == 0 else x].astype(F32)
        for d in (1, 2, 3):
            total += rs2[k, ys(d) if k == 0 else xs(d)].astype(F32)
        sums.append(total.astype(BF))
    ob[...] = dot(expand, jnp.concatenate(sums, axis=0)).astype(BF).reshape(2, NX, NY, ROWS, COL)

    def back(i):
        px, py, pc = partner(i)
        return pltpu.make_async_remote_copy(
            src_ref=ob.at[pc, px, py], dst_ref=rb.at[c, x, y], send_sem=bsem.at[i],
            recv_sem=brsem.at[i], device_id=dev(r, px, py, pc), device_id_type=MESH,
        )

    @pl.loop(1, PLANE)
    def _(i):
        back(i).start()

    rb[c, x, y] = ob[c, x, y]
    zstep(1, 4)

    for cp in q2:
        cp.wait_recv()
    q3 = send(ds.at[c], ds.at[c], sib)

    unpick = jnp.zeros((TOK, ROWS), F32)
    for k in range(2):
        bt = hot(ch_row[k] - e * TOK == iota((TOK, CAP), 0))
        at = hot(pos_col[k] - my_first == iota((CAP, ROWS), 1))
        unpick += dot(bt, at)
    unpick_ref[...] = unpick.astype(BF)

    for cp in g2:
        cp.wait_recv()
    total = (gy[0] + gy[1]) + (gy[2] + gy[3])
    for k in range(2):
        dgate_ref[0, k : k + 1, :] = total[k, 0:1, :]

    zstep(0, 5)
    zstep(1, 5)
    q3.wait_recv()
    for k in range(2):
        act = zb[0, :, k].reshape(NZ * CAP, F)
        dh = zb[1, :, k].reshape(NZ * CAP, F)

        def cols(a, j, h):
            return jnp.concatenate(
                [ds[a, 2 * k : 2 * k + 2, :, g, j, h].reshape(CAP, COL) for g in range(NZ)], axis=0
            )

        for j in range(2):
            xk = jnp.concatenate([cols(0, j, h) for h in range(2)], axis=1)
            sk = jnp.concatenate([cols(1, j, h) for h in range(2)], axis=1)
            dwin_ref[k, j * 256 : (j + 1) * 256, :] = dot(xk, dh, 0, 0).astype(BF)
            dwout_ref[k, :, j * 256 : (j + 1) * 256] = dot(act, sk, 0, 0).astype(BF)

    @pl.loop(1, PLANE)
    def _(i):
        back(i).wait_recv()

    rows_ref[...] = rb[...]

    assert counter[0] <= NSEM, counter[0]
    for cp in sent:
        cp.wait_send()

    @pl.loop(1, PLANE)
    def _(i):
        forth(i).wait_send()
        back(i).wait_send()


def finish(rows_ref, unpick_ref, gate_ref, win_ref, wout_ref, dtok_ref, dgate_ref, dwin_ref, dwout_ref, sem):
    copies = [
        pltpu.make_async_copy(win_ref, dwin_ref, sem.at[0]),
        pltpu.make_async_copy(wout_ref, dwout_ref, sem.at[1]),
    ]
    for cp in copies:
        cp.start()
    dgate_ref[...] = gate_ref[...]
    for i in range(NX):
        rows = jnp.concatenate([rows_ref[h, i, j] for j in range(NY) for h in range(2)], axis=1)
        dtok_ref[0, :, i * BLK : (i + 1) * BLK] = dot(unpick_ref[...], rows).astype(BF)
    for cp in copies:
        cp.wait()


def local(tokens, grad_out, gates, chosen, w_in, w_out):
    hbm = pl.BlockSpec(memory_space=pl.ANY)
    vmem = pl.BlockSpec(memory_space=pltpu.VMEM)
    dma = pltpu.SemaphoreType.DMA
    d_gate = jax.ShapeDtypeStruct((1, 2, CAP), F32)
    d_in = jax.ShapeDtypeStruct((2, D // NZ, F), BF)
    d_out = jax.ShapeDtypeStruct((2, F, D // NZ), BF)
    parts = pl.pallas_call(
        kernel,
        out_shape=(
            jax.ShapeDtypeStruct((2, NX, NY, ROWS, COL), BF),
            jax.ShapeDtypeStruct((TOK, ROWS), BF),
            d_gate,
            d_in,
            d_out,
        ),
        in_specs=[hbm, hbm, vmem, vmem, hbm, hbm],
        out_specs=(vmem,) * 5,
        scratch_shapes=[
            pltpu.VMEM((TOK, D), BF),
            pltpu.VMEM((TOK, D), BF),
            pltpu.VMEM((2, D, F), BF),
            pltpu.VMEM((2, F, D), BF),
            pltpu.VMEM((2, NX, NY, 2, ROWS, COL), BF),
            pltpu.VMEM((2, NX, NY, 2, ROWS, COL), BF),
            pltpu.VMEM((2, 2, 2, NX, NY, CAP, COL), BF),
            pltpu.VMEM((NX * NY, ROWS, COL), F32),
            pltpu.VMEM((NX, NY, 2, ROWS, COL), BF),
            pltpu.VMEM((2, NX, NY, NZ, 2, 2, ROWS, COL), BF),
            pltpu.VMEM((2, NZ, 2, CAP, F), BF),
            pltpu.VMEM((2, 2, CAP, F), F32),
            pltpu.VMEM((2, 2, NX, NY, CAP, COL), BF),
            pltpu.VMEM((2, NX, NY, CAP, COL), BF),
            pltpu.VMEM((2, 4, 4, CAP, COL), BF),
            pltpu.VMEM((2, 4, CAP, COL), BF),
            pltpu.VMEM((2, 4, CAP, COL), BF),
            pltpu.VMEM((2, NX, NY, ROWS, COL), BF),
            pltpu.VMEM((2, NX, NY, ROWS, COL), BF),
            pltpu.VMEM((3, 2, 8, CAP), F32),
            pltpu.VMEM((2, 8, CAP), F32),
            pltpu.VMEM((4, 2, 8, CAP), F32),
            pltpu.VMEM((4, 2, 8, CAP), F32),
            dma((NSEM,)),
            dma((NSEM,)),
            dma((PLANE,)),
            dma((PLANE,)),
            dma((PLANE,)),
            dma((PLANE,)),
            dma((4,)),
        ],
        compiler_params=pltpu.CompilerParams(
            collective_id=0, has_side_effects=True, vmem_limit_bytes=60 << 20
        ),
        name="expert_backward",
    )(tokens, grad_out, gates, chosen, w_in, w_out)
    return pl.pallas_call(
        finish,
        out_shape=(jax.ShapeDtypeStruct((1, TOK, D), BF), d_gate, d_in, d_out),
        in_specs=[vmem, vmem, vmem, hbm, hbm],
        out_specs=(vmem, vmem, hbm, hbm),
        scratch_shapes=[dma((2,))],
        compiler_params=pltpu.CompilerParams(vmem_limit_bytes=60 << 20),
        name="finish",
    )(*parts)


def solution(mesh):
    return jax.shard_map(
        local,
        mesh=mesh,
        in_specs=(
            P("rep", "exp", None),
            P("rep", "exp", None),
            P("rep", None, None),
            P("rep", None, None),
            P(None, None, "exp"),
            P(None, "exp", None),
        ),
        out_specs=(
            P("rep", "exp", None),
            P("rep", None, None),
            P(None, "rep", "exp"),
            P(None, "exp", "rep"),
        ),
        check_vma=False,
    )
```

```python
import jax
import jax.numpy as jnp
from jax import lax
from jax.experimental import pallas as pl
from jax.experimental.pallas import tpu as pltpu
from jax.sharding import PartitionSpec as P

GELU_SCALE = 0.7978845608028654
GELU_CUBIC = 0.044715

BF = jnp.bfloat16
F32 = jnp.float32
MESH = pl.DeviceIdType.MESH

NX, NY, NZ = 4, 4, 8
D = 4096
F = 256
CAP = 128
TOK = 128
MOST = 8
ROWS = 2 * MOST
PAD = NX * NY * 2 * ROWS
COL = 128
BLK = D // NX
PLANE = NX * NY * 2

NSEM = 144


def dot(a, b, ca=1, cb=0):
    return lax.dot_general(a, b, (((ca,), (cb,)), ((), ())), preferred_element_type=F32)


def kernel(
    tok_hbm, grad_hbm, gates_ref, chosen_ref, win_hbm, wout_hbm,
    rows_ref, unpick_ref, dgate_ref, dwin_ref, dwout_ref,
    tok, grad, win, wout, pk, rp, xc, gc, eb, ds, zb, acc, ps, rsib, rs1, ts, rs2, ob, rb,
    gbuf, gsib, gx, gy,
    ssem, rsem, asem, arsem, bsem, brsem, lsem,
):
    r = lax.axis_index("rep")
    e = lax.axis_index("exp")
    x = e // 8
    y = (e // 2) % 4
    c = e % 2
    oc = 1 - c
    chip = x * NY + y

    def dev(rr, xx, yy, c_):
        return (rr, (xx * 4 + yy) * 2 + c_)

    def xs(d):
        return lax.rem(x + d, 4)

    def ys(d):
        return lax.rem(y + d, 4)

    def zs(d):
        return lax.rem(r + d, 8)

    sib = dev(r, x, y, oc)

    loads = [
        pltpu.make_async_copy(tok_hbm.at[0], tok, lsem.at[0]),
        pltpu.make_async_copy(grad_hbm.at[0], grad, lsem.at[1]),
        pltpu.make_async_copy(win_hbm, win, lsem.at[2]),
        pltpu.make_async_copy(wout_hbm, wout, lsem.at[3]),
    ]
    loads[0].start()
    loads[1].start()

    barrier = pltpu.get_barrier_semaphore()

    for i in range(1, PLANE):
        to = dev(r, xs(i // 8), ys((i // 2) % 4), oc if i % 2 else c)
        pl.semaphore_signal(barrier, inc=1, device_id=to, device_id_type=MESH)
    for d in range(1, NZ):
        pl.semaphore_signal(barrier, inc=1, device_id=dev(zs(d), x, y, c), device_id_type=MESH)

    counter = [0]
    sent = []

    def send(src, dst, to):
        i = counter[0]
        counter[0] += 1
        cp = pltpu.make_async_remote_copy(
            src_ref=src, dst_ref=dst, send_sem=ssem.at[i], recv_sem=rsem.at[i],
            device_id=to, device_id_type=MESH,
        )
        cp.start()
        sent.append(cp)
        return cp

    def iota(shape, dim):
        return lax.broadcasted_iota(jnp.int32, shape, dim)

    def hot(m):
        return jnp.where(m, 1.0, 0.0).astype(BF)

    sq = (CAP, CAP)
    my_first = (c * (NX * NY) + chip) * ROWS
    ch_row, ch_col, pos_row, pos_col, gate_col = [], [], [], [], []
    for k in range(2):
        row = chosen_ref[0, k : k + 1, :]
        rb_ = jnp.broadcast_to(row, sq)
        cb_ = rb_.T
        same = (rb_ // TOK) == (cb_ // TOK)
        rank_col = jnp.sum(jnp.where(same & (iota(sq, 1) < iota(sq, 0)), 1, 0), axis=1, keepdims=True)
        rank_row = jnp.sum(jnp.where(same & (iota(sq, 0) < iota(sq, 1)), 1, 0), axis=0, keepdims=True)

        def place(own, rank):
            return ((own % 2) * (NX * NY) + own // 2) * ROWS + k * MOST + rank

        ch_row.append(row)
        ch_col.append(cb_[:, 0:1])
        pos_row.append(place(row // TOK, rank_row))
        pos_col.append(place(cb_[:, 0:1] // TOK, rank_col))

    pick = jnp.zeros((ROWS, TOK), F32)
    for k in range(2):
        a = hot(pos_row[k] - my_first == iota((ROWS, CAP), 0))
        b = hot(ch_col[k] - e * TOK == iota((CAP, TOK), 1))
        pick += dot(a, b)
    pick = pick.astype(BF)

    loads[0].wait()
    loads[1].wait()
    loads[2].start()
    loads[3].start()

    @pl.loop(0, NX)
    def _(i):
        cols = pl.ds(pl.multiple_of(i * BLK, BLK), BLK)
        xr = dot(pick, tok[:, cols]).astype(BF)
        dr = dot(pick, grad[:, cols]).astype(BF)
        for j in range(NY):
            for k in range(2):
                at = slice((2 * j + k) * COL, (2 * j + k + 1) * COL)
                pk[k, i, j, 0] = xr[:, at]
                pk[k, i, j, 1] = dr[:, at]

    pl.semaphore_wait(barrier, PLANE - 1 + NZ - 1)

    def plane(src, dst, s_sem, r_sem):
        copies = []
        for i in range(1, PLANE):
            px, py, pc = xs(i // 8), ys((i // 2) % 4), (oc if i % 2 else c)
            cp = pltpu.make_async_remote_copy(
                src_ref=src.at[pc, px, py], dst_ref=dst.at[c, x, y], send_sem=s_sem.at[i],
                recv_sem=r_sem.at[i], device_id=dev(r, px, py, pc), device_id_type=MESH,
            )
            cp.start()
            copies.append(cp)
        return copies

    forth = plane(pk, rp, asem, arsem)
    rp[c, x, y] = pk[c, x, y]
    gather = jnp.concatenate([hot(pos_col[k] == iota((CAP, PAD), 1)) for k in range(2)], axis=0)
    for k in range(2):
        gate_col.append(jnp.broadcast_to(gates_ref[0, k : k + 1, :], sq).T)
        gc[k * 8 : (k + 1) * 8] = gate_col[k].reshape(8, ROWS, COL)

    for cp in forth:
        cp.wait_recv()

    both = jnp.concatenate([rp[:, :, :, k].reshape(PAD, COL) for k in range(2)], axis=1)
    both = dot(gather, both).astype(BF)
    for a in range(2):
        for k in range(2):
            xc[a, k, c, x, y] = both[k * CAP : (k + 1) * CAP, a * COL : (a + 1) * COL]

    class Spread:
        def __init__(self, row):
            self.row = row

        def block(self, k):
            return self.row(k, 0, x if k == 0 else y)

        def first(self):
            self.got = []
            for d in (1, 3, 2):
                for k, to in ((0, dev(r, xs(d), y, c)), (1, dev(r, x, ys(d), c))):
                    ref = self.block(k)
                    self.got.append(send(ref, ref, to))

        def along(self, k, d):
            return dev(r, x, ys(d), c) if k == 0 else dev(r, xs(d), y, c)

        def second(self):
            for cp in self.got:
                cp.wait_recv()
            self.got = []
            for k in range(2):
                ref = self.row(k, 0, slice(0, 4))
                for d in (1, 3):
                    self.got.append(send(ref, ref, self.along(k, d)))
            self.sibs = [send(self.row(k, 0, slice(0, 4)), self.row(k, 0, slice(0, 4)), sib) for k in range(2)]

        def forward(self):
            got, self.got = self.got, []
            for k in range(2):
                for n, (d, at) in enumerate(((3, slice(0, 2)), (1, slice(2, 4)))):
                    got[2 * k + n].wait_recv()
                    ref = self.row(k, d, at)
                    self.got.append(send(ref, ref, self.along(k, 1 if d == 3 else 3)))
            for k in range(2):
                for d in (3, 1):
                    ref = self.row(k, d, slice(0, 4))
                    self.sibs.append(send(ref, ref, sib))

        def last(self):
            for cp in self.got:
                cp.wait_recv()
            for k in range(2):
                ref = self.row(k, 2, slice(0, 4))
                self.sibs.append(send(ref, ref, sib))

        def done(self):
            for cp in self.sibs:
                cp.wait_recv()

    def rows_of(a):
        return lambda k, d, at: xc.at[a, 0, c, at, ys(d)] if k == 0 else xc.at[a, 1, c, xs(d), at]

    def columns_of(a):
        return lambda k, d, at: ds.at[a, c, at, ys(d), 0:4] if k == 0 else ds.at[a, c, xs(d), at, 4:8]

    own_rows = [Spread(rows_of(a)) for a in range(2)]
    all_rows = [Spread(columns_of(a)) for a in range(2)]
    for sp in own_rows:
        sp.first()
    for sp in own_rows:
        sp.second()
    loads[2].wait()
    loads[3].wait()
    for sp in own_rows:
        sp.forward()

    slots = pl.ds(pl.multiple_of(lax.rem(chip, 8) * ROWS, ROWS), ROWS)

    def two(to):
        return pl.ds(2 * lax.rem(to, 2), 2)

    def exchange(a, src):
        copies = []
        for d in (1, 7, 2, 6, 3, 5, 4):
            copies.append(send(src(zs(d)), ds.at[a, c, x, y, r], dev(zs(d), x, y, c)))
        return copies

    right, left = dev(zs(1), x, y, c), dev(zs(7), x, y, c)
    ring = [None, None]

    def zstep(w, s):
        if s > 1:
            for cp in ring[w]:
                cp.wait_recv()
        if s < 4:
            ra, la = zb.at[w, zs(9 - s)], zb.at[w, zs(s - 1)]
        elif s == 4:
            ra, la = zb.at[w, zs(5), 0], zb.at[w, zs(3), 1]
        else:
            return
        ring[w] = [send(ra, ra, right), send(la, la, left)]

    acc[...] = jnp.zeros_like(acc)
    acts, dhs = [], []
    for a in range(2):
        own_rows[a].last()
        if a == 0:
            ex0 = exchange(0, lambda to: xc.at[0, x // 2, c, to // 2, two(to), slots])
            ds[0, c, x, y, r] = xc[0, x // 2, c, r // 2, two(r), slots, :]
        own_rows[a].done()

        @pl.loop(0, NX)
        def _(i):
            cols = pl.ds(pl.multiple_of(i * BLK, BLK), BLK)
            for k in range(2):
                lhs = jnp.concatenate(
                    [xc[a, k, h, i, j] for j in range(NY) for h in range(2)], axis=1
                )
                if a == 0:
                    acc[0, k] += dot(lhs, win[k, cols, :])
                else:
                    acc[1, k] += dot(lhs, wout[k, :, cols], 1, 1)

        if a == 0:
            for k in range(2):
                hidden = acc[0, k]
                tang = jnp.tanh(GELU_SCALE * (hidden + GELU_CUBIC * hidden * hidden * hidden))
                acts.append((0.5 * hidden * (1.0 + tang)).astype(BF))
                slope = 0.5 * (1.0 + tang) + 0.5 * hidden * (1.0 - tang * tang) * GELU_SCALE * (
                    1.0 + 3.0 * GELU_CUBIC * hidden * hidden
                )
                acc[0, k] = slope
                zb[0, r, k] = acts[k]
            zstep(0, 1)
            for cp in ex0:
                cp.wait_recv()
            all_rows[0].first()
    for k in range(2):
        dhs.append((gate_col[k][:, 0:1] * acc[1, k] * acc[0, k]).astype(BF))
        zb[1, r, k] = dhs[k]
    zstep(1, 1)
    zstep(0, 2)
    for k in range(2):
        gbuf[0, k] = lax.dot_general(
            jnp.ones((8, F), F32), zb[0, r, k].astype(F32) * acc[1, k], (((1,), (1,)), ((), ())),
            precision=lax.Precision.HIGHEST, preferred_element_type=F32,
        )
    g0 = send(gbuf.at[0], gsib, sib)


    @pl.loop(0, NX)
    def _(i):
        for j in range(NY):
            eb[i, j] = (gc[chip] * xc[1, x // 2, c, i, j, slots, :].astype(F32)).astype(BF)

    ex1 = exchange(1, lambda to: eb.at[to // 2, two(to)])
    ds[1, c, x, y, r] = eb[r // 2, two(r)]

    pair = []
    for k in range(2):

        @pl.loop(0, NX)
        def _(i):
            cols = pl.ds(pl.multiple_of(i * BLK, BLK), BLK)
            part = dot(zb[1, r, k], win[k, cols, :], 1, 1).astype(BF)
            for j in range(NY):
                for h in range(2):
                    ps[k, h, i, j] = part[:, (2 * j + h) * COL : (2 * j + h + 1) * COL]

        pair.append(send(ps.at[k, oc], rsib.at[k], sib))
        if k == 0:
            all_rows[0].second()

    all_rows[0].forward()
    zstep(1, 2)

    stage1 = [[], []]
    for k in range(2):
        pair[k].wait_recv()

        @pl.loop(0, NX)
        def _(i):
            for j in range(NY):
                ps[k, c, i, j] = (ps[k, c, i, j].astype(F32) + rsib[k, i, j].astype(F32)).astype(BF)

        for d in (1, 3, 2):
            if k == 0:
                stage1[k].append(send(ps.at[0, c, xs(d)], rs1.at[0, x], dev(r, xs(d), y, c)))
            else:
                stage1[k].append(send(ps.at[1, c, :, ys(d)], rs1.at[1, y], dev(r, x, ys(d), c)))

    zstep(0, 3)

    g0.wait_recv()
    gbuf[1] = gbuf[0] + gsib[...]
    gx[x] = gbuf[1]
    g1 = [send(gbuf.at[1], gx.at[x], dev(r, xs(d), y, c)) for d in (1, 3, 2)]

    for cp in ex1:
        cp.wait_recv()
    all_rows[1].first()
    all_rows[0].last()
    zstep(1, 3)

    stage2 = [[], []]
    for k in range(2):
        for cp in stage1[k]:
            cp.wait_recv()
        for j in range(4):
            total = (ps[0, c, x, j] if k == 0 else ps[1, c, j, y]).astype(F32)
            for d in (1, 2, 3):
                total += rs1[k, xs(d) if k == 0 else ys(d), j].astype(F32)
            ts[k, j] = total.astype(BF)
        for d in (1, 3, 2):
            if k == 0:
                stage2[k].append(send(ts.at[0, ys(d)], rs2.at[0, y], dev(r, x, ys(d), c)))
            else:
                stage2[k].append(send(ts.at[1, xs(d)], rs2.at[1, x], dev(r, xs(d), y, c)))

    all_rows[1].second()
    zstep(0, 4)
    for cp in g1:
        cp.wait_recv()
    gbuf[2] = (gx[0] + gx[1]) + (gx[2] + gx[3])
    gy[y] = gbuf[2]
    g2 = [send(gbuf.at[2], gy.at[y], dev(r, x, ys(d), c)) for d in (1, 3, 2)]

    expand = jnp.concatenate([hot(pos_row[k] == iota((PAD, CAP), 0)) for k in range(2)], axis=1)
    sums = []
    for k in range(2):
        for cp in stage2[k]:
            cp.wait_recv()
        total = ts[k, y if k == 0 else x].astype(F32)
        for d in (1, 2, 3):
            total += rs2[k, ys(d) if k == 0 else xs(d)].astype(F32)
        sums.append(total.astype(BF))
    ob[...] = dot(expand, jnp.concatenate(sums, axis=0)).astype(BF).reshape(2, NX, NY, ROWS, COL)

    back = plane(ob, rb, bsem, brsem)
    rb[c, x, y] = ob[c, x, y]
    zstep(1, 4)

    all_rows[1].forward()

    unpick = jnp.zeros((TOK, ROWS), F32)
    for k in range(2):
        bt = hot(ch_row[k] - e * TOK == iota((TOK, CAP), 0))
        at = hot(pos_col[k] - my_first == iota((CAP, ROWS), 1))
        unpick += dot(bt, at)
    unpick_ref[...] = unpick.astype(BF)

    for cp in g2:
        cp.wait_recv()
    total = (gy[0] + gy[1]) + (gy[2] + gy[3])
    for k in range(2):
        dgate_ref[0, k : k + 1, :] = total[k, 0:1, :]

    all_rows[1].last()
    zstep(0, 5)
    zstep(1, 5)
    for sp in all_rows:
        sp.done()
    for k in range(2):
        act = zb[0, :, k].reshape(NZ * CAP, F)
        dh = zb[1, :, k].reshape(NZ * CAP, F)

        def cols(a, j, h):
            return jnp.concatenate(
                [ds[a, h, 2 * k : 2 * k + 2, :, g, j].reshape(CAP, COL) for g in range(NZ)], axis=0
            )

        for j in range(2):
            xk = jnp.concatenate([cols(0, j, h) for h in range(2)], axis=1)
            sk = jnp.concatenate([cols(1, j, h) for h in range(2)], axis=1)
            dwin_ref[k, j * 256 : (j + 1) * 256, :] = dot(xk, dh, 0, 0).astype(BF)
            dwout_ref[k, :, j * 256 : (j + 1) * 256] = dot(act, sk, 0, 0).astype(BF)

    for cp in back:
        cp.wait_recv()
    rows_ref[...] = rb[...]

    assert counter[0] <= NSEM, counter[0]
    for cp in sent:
        cp.wait_send()

    for cp in forth + back:
        cp.wait_send()


def finish(rows_ref, unpick_ref, gate_ref, win_ref, wout_ref, dtok_ref, dgate_ref, dwin_ref, dwout_ref):
    for i in range(NX):
        rows = jnp.concatenate([rows_ref[h, i, j] for j in range(NY) for h in range(2)], axis=1)
        dtok_ref[0, :, i * BLK : (i + 1) * BLK] = dot(unpick_ref[...], rows).astype(BF)
    dgate_ref[...] = gate_ref[...]
    dwin_ref[...] = win_ref[...]
    dwout_ref[...] = wout_ref[...]


def local(tokens, grad_out, gates, chosen, w_in, w_out):
    hbm = pl.BlockSpec(memory_space=pl.ANY)
    vmem = pl.BlockSpec(memory_space=pltpu.VMEM)
    dma = pltpu.SemaphoreType.DMA
    d_gate = jax.ShapeDtypeStruct((1, 2, CAP), F32)
    d_in = jax.ShapeDtypeStruct((2, D // NZ, F), BF)
    d_out = jax.ShapeDtypeStruct((2, F, D // NZ), BF)
    parts = pl.pallas_call(
        kernel,
        out_shape=(
            jax.ShapeDtypeStruct((2, NX, NY, ROWS, COL), BF),
            jax.ShapeDtypeStruct((TOK, ROWS), BF),
            d_gate,
            d_in,
            d_out,
        ),
        in_specs=[hbm, hbm, vmem, vmem, hbm, hbm],
        out_specs=(vmem,) * 5,
        scratch_shapes=[
            pltpu.VMEM((TOK, D), BF),
            pltpu.VMEM((TOK, D), BF),
            pltpu.VMEM((2, D, F), BF),
            pltpu.VMEM((2, F, D), BF),
            pltpu.VMEM((2, NX, NY, 2, ROWS, COL), BF),
            pltpu.VMEM((2, NX, NY, 2, ROWS, COL), BF),
            pltpu.VMEM((2, 2, 2, NX, NY, CAP, COL), BF),
            pltpu.VMEM((NX * NY, ROWS, COL), F32),
            pltpu.VMEM((NX, NY, ROWS, COL), BF),
            pltpu.VMEM((2, 2, NX, NY, NZ, 2, ROWS, COL), BF),
            pltpu.VMEM((2, NZ, 2, CAP, F), BF),
            pltpu.VMEM((2, 2, CAP, F), F32),
            pltpu.VMEM((2, 2, NX, NY, CAP, COL), BF),
            pltpu.VMEM((2, NX, NY, CAP, COL), BF),
            pltpu.VMEM((2, 4, 4, CAP, COL), BF),
            pltpu.VMEM((2, 4, CAP, COL), BF),
            pltpu.VMEM((2, 4, CAP, COL), BF),
            pltpu.VMEM((2, NX, NY, ROWS, COL), BF),
            pltpu.VMEM((2, NX, NY, ROWS, COL), BF),
            pltpu.VMEM((3, 2, 8, CAP), F32),
            pltpu.VMEM((2, 8, CAP), F32),
            pltpu.VMEM((4, 2, 8, CAP), F32),
            pltpu.VMEM((4, 2, 8, CAP), F32),
            dma((NSEM,)),
            dma((NSEM,)),
            dma((PLANE,)),
            dma((PLANE,)),
            dma((PLANE,)),
            dma((PLANE,)),
            dma((4,)),
        ],
        compiler_params=pltpu.CompilerParams(
            collective_id=0, has_side_effects=True, vmem_limit_bytes=60 << 20
        ),
        name="expert_backward",
    )(tokens, grad_out, gates, chosen, w_in, w_out)
    return pl.pallas_call(
        finish,
        out_shape=(jax.ShapeDtypeStruct((1, TOK, D), BF), d_gate, d_in, d_out),
        in_specs=[vmem] * 5,
        out_specs=(vmem,) * 4,
        compiler_params=pltpu.CompilerParams(vmem_limit_bytes=60 << 20),
        name="finish",
    )(*parts)


def solution(mesh):
    return jax.shard_map(
        local,
        mesh=mesh,
        in_specs=(
            P("rep", "exp", None),
            P("rep", "exp", None),
            P("rep", None, None),
            P("rep", None, None),
            P(None, None, "exp"),
            P(None, "exp", None),
        ),
        out_specs=(
            P("rep", "exp", None),
            P("rep", None, None),
            P(None, "rep", "exp"),
            P(None, "exp", "rep"),
        ),
        check_vma=False,
    )
```

```python
import jax
import jax.numpy as jnp
from jax import lax
from jax.experimental import pallas as pl
from jax.experimental.pallas import tpu as pltpu
from jax.sharding import PartitionSpec as P

GELU_SCALE = 0.7978845608028654
GELU_CUBIC = 0.044715

BF = jnp.bfloat16
F32 = jnp.float32
MESH = pl.DeviceIdType.MESH

NX, NY, NZ = 4, 4, 8
D = 4096
F = 256
CAP = 128
TOK = 128
MOST = 8
ROWS = 2 * MOST
PAD = NX * NY * 2 * ROWS
COL = 128
BLK = D // NX
PLANE = NX * NY * 2

NSEM = 144


def dot(a, b, ca=1, cb=0):
    return lax.dot_general(a, b, (((ca,), (cb,)), ((), ())), preferred_element_type=F32)


def kernel(
    tok_hbm, grad_hbm, gates_ref, chosen_ref, win_hbm, wout_hbm,
    rows_ref, unpick_ref, dgate_ref, dwin_ref, dwout_ref,
    tok, grad, win, wout, pk, rp, xc, gc, eb, ds, zb, acc, ps, rsib, rs1, ts, rs2, ob, rb,
    gbuf, gsib, gx, gy,
    ssem, rsem, asem, arsem, bsem, brsem, lsem,
):
    r = lax.axis_index("rep")
    e = lax.axis_index("exp")
    x = e // 8
    y = (e // 2) % 4
    c = e % 2
    oc = 1 - c
    chip = x * NY + y

    def dev(rr, xx, yy, c_):
        return (rr, (xx * 4 + yy) * 2 + c_)

    def xs(d):
        return lax.rem(x + d, 4)

    def ys(d):
        return lax.rem(y + d, 4)

    def zs(d):
        return lax.rem(r + d, 8)

    sib = dev(r, x, y, oc)

    loads = [
        pltpu.make_async_copy(tok_hbm.at[0], tok, lsem.at[0]),
        pltpu.make_async_copy(grad_hbm.at[0], grad, lsem.at[1]),
        pltpu.make_async_copy(win_hbm, win, lsem.at[2]),
        pltpu.make_async_copy(wout_hbm, wout, lsem.at[3]),
    ]
    loads[0].start()
    loads[1].start()

    barrier = pltpu.get_barrier_semaphore()

    for i in range(1, PLANE):
        to = dev(r, xs(i // 8), ys((i // 2) % 4), oc if i % 2 else c)
        pl.semaphore_signal(barrier, inc=1, device_id=to, device_id_type=MESH)
    for d in range(1, NZ):
        pl.semaphore_signal(barrier, inc=1, device_id=dev(zs(d), x, y, c), device_id_type=MESH)

    counter = [0]
    sent = []

    def send(src, dst, to):
        i = counter[0]
        counter[0] += 1
        cp = pltpu.make_async_remote_copy(
            src_ref=src, dst_ref=dst, send_sem=ssem.at[i], recv_sem=rsem.at[i],
            device_id=to, device_id_type=MESH,
        )
        cp.start()
        sent.append(cp)
        return cp

    def iota(shape, dim):
        return lax.broadcasted_iota(jnp.int32, shape, dim)

    def hot(m):
        return jnp.where(m, 1.0, 0.0).astype(BF)

    sq = (CAP, CAP)
    my_first = (c * (NX * NY) + chip) * ROWS
    ch_row, ch_col, pos_row, pos_col, gate_col = [], [], [], [], []
    for k in range(2):
        row = chosen_ref[0, k : k + 1, :]
        rb_ = jnp.broadcast_to(row, sq)
        cb_ = rb_.T
        same = (rb_ // TOK) == (cb_ // TOK)
        rank_col = jnp.sum(jnp.where(same & (iota(sq, 1) < iota(sq, 0)), 1, 0), axis=1, keepdims=True)
        rank_row = jnp.sum(jnp.where(same & (iota(sq, 0) < iota(sq, 1)), 1, 0), axis=0, keepdims=True)

        def place(own, rank):
            return ((own % 2) * (NX * NY) + own // 2) * ROWS + k * MOST + rank

        ch_row.append(row)
        ch_col.append(cb_[:, 0:1])
        pos_row.append(place(row // TOK, rank_row))
        pos_col.append(place(cb_[:, 0:1] // TOK, rank_col))

    pick = jnp.zeros((ROWS, TOK), F32)
    for k in range(2):
        a = hot(pos_row[k] - my_first == iota((ROWS, CAP), 0))
        b = hot(ch_col[k] - e * TOK == iota((CAP, TOK), 1))
        pick += dot(a, b)
    pick = pick.astype(BF)

    loads[0].wait()
    loads[1].wait()
    loads[2].start()
    loads[3].start()

    @pl.loop(0, NX)
    def _(i):
        cols = pl.ds(pl.multiple_of(i * BLK, BLK), BLK)
        xr = dot(pick, tok[:, cols]).astype(BF)
        dr = dot(pick, grad[:, cols]).astype(BF)
        for j in range(NY):
            for k in range(2):
                at = slice((2 * j + k) * COL, (2 * j + k + 1) * COL)
                pk[k, i, j, 0] = xr[:, at]
                pk[k, i, j, 1] = dr[:, at]

    pl.semaphore_wait(barrier, PLANE - 1 + NZ - 1)

    def plane(src, dst, s_sem, r_sem):
        copies = []
        for i in range(1, PLANE):
            px, py, pc = xs(i // 8), ys((i // 2) % 4), (oc if i % 2 else c)
            cp = pltpu.make_async_remote_copy(
                src_ref=src.at[pc, px, py], dst_ref=dst.at[c, x, y], send_sem=s_sem.at[i],
                recv_sem=r_sem.at[i], device_id=dev(r, px, py, pc), device_id_type=MESH,
            )
            cp.start()
            copies.append(cp)
        return copies

    forth = plane(pk, rp, asem, arsem)
    rp[c, x, y] = pk[c, x, y]
    gather = jnp.concatenate([hot(pos_col[k] == iota((CAP, PAD), 1)) for k in range(2)], axis=0)
    for k in range(2):
        gate_col.append(jnp.broadcast_to(gates_ref[0, k : k + 1, :], sq).T)
        gc[k * 8 : (k + 1) * 8] = gate_col[k].reshape(8, ROWS, COL)

    for cp in forth:
        cp.wait_recv()

    both = jnp.concatenate([rp[:, :, :, k].reshape(PAD, COL) for k in range(2)], axis=1)
    both = dot(gather, both).astype(BF)
    for a in range(2):
        for k in range(2):
            xc[a, k, c, x, y] = both[k * CAP : (k + 1) * CAP, a * COL : (a + 1) * COL]

    class Spread:
        def __init__(self, row):
            self.row = row

        def block(self, k):
            return self.row(k, 0, x if k == 0 else y)

        def first(self):
            self.got = []
            for d in (1, 3, 2):
                for k, to in ((0, dev(r, xs(d), y, c)), (1, dev(r, x, ys(d), c))):
                    ref = self.block(k)
                    self.got.append(send(ref, ref, to))

        def along(self, k, d):
            return dev(r, x, ys(d), c) if k == 0 else dev(r, xs(d), y, c)

        def second(self):
            for cp in self.got:
                cp.wait_recv()
            self.got = []
            for k in range(2):
                ref = self.row(k, 0, slice(0, 4))
                for d in (1, 3):
                    self.got.append(send(ref, ref, self.along(k, d)))
            self.sibs = {}
            self.share(0)

        def forward(self):
            got, self.got = self.got, []
            for k in range(2):
                for n, (d, at) in enumerate(((3, slice(0, 2)), (1, slice(2, 4)))):
                    got[2 * k + n].wait_recv()
                    ref = self.row(k, d, at)
                    self.got.append(send(ref, ref, self.along(k, 1 if d == 3 else 3)))
            self.share(3)
            self.share(1)

        def share(self, d):
            refs = [self.row(k, d, slice(0, 4)) for k in range(2)]
            self.sibs[d] = [send(ref, ref, sib) for ref in refs]

        def last(self):
            for cp in self.got:
                cp.wait_recv()
            self.share(2)

        def done(self, rows=(0, 3, 1, 2)):
            for d in rows:
                for cp in self.sibs[d]:
                    cp.wait_recv()

    def rows_of(a):
        return lambda k, d, at: xc.at[a, 0, c, at, ys(d)] if k == 0 else xc.at[a, 1, c, xs(d), at]

    def columns_of(a):
        return lambda k, d, at: ds.at[a, c, at, ys(d), 0:4] if k == 0 else ds.at[a, c, xs(d), at, 4:8]

    own_rows = [Spread(rows_of(a)) for a in range(2)]
    all_rows = [Spread(columns_of(a)) for a in range(2)]
    slots = pl.ds(pl.multiple_of(lax.rem(chip, 8) * ROWS, ROWS), ROWS)

    def two(to):
        return pl.ds(2 * lax.rem(to, 2), 2)

    def exchange(a, src):
        copies = []
        for d in (1, 7, 2, 6, 3, 5, 4):
            copies.append(send(src(zs(d)), ds.at[a, c, x, y, r], dev(zs(d), x, y, c)))
        return copies

    right, left = dev(zs(1), x, y, c), dev(zs(7), x, y, c)
    ring = [None, None]

    def zstep(w, s):
        if s > 1:
            for cp in ring[w]:
                cp.wait_recv()
        if s < 4:
            ra, la = zb.at[w, zs(9 - s)], zb.at[w, zs(s - 1)]
        elif s == 4:
            ra, la = zb.at[w, zs(5), 0], zb.at[w, zs(3), 1]
        else:
            return
        ring[w] = [send(ra, ra, right), send(la, la, left)]

    def step(a, d):
        own_rows[a].done((d,))
        for k in range(2):
            total = None
            for j in range(4):
                px, py = (j, ys(d)) if k == 0 else (xs(d), j)
                lhs = jnp.concatenate([xc[a, k, h, px, py] for h in range(2)], axis=1)
                cols = pl.ds(pl.multiple_of((px * NY + py) * 2 * COL, 2 * COL), 2 * COL)
                part = dot(lhs, win[k, cols, :]) if a == 0 else dot(lhs, wout[k, :, cols], 1, 1)
                total = part if total is None else total + part
            acc[a, k] = total if d == 0 else acc[a, k] + total

    for sp in own_rows:
        sp.first()
    for sp in own_rows:
        sp.second()
    loads[2].wait()
    loads[3].wait()
    step(0, 0)
    own_rows[0].forward()
    step(1, 0)
    own_rows[1].forward()
    step(0, 3)
    step(0, 1)
    own_rows[0].last()
    ex0 = exchange(0, lambda to: xc.at[0, x // 2, c, to // 2, two(to), slots])
    ds[0, c, x, y, r] = xc[0, x // 2, c, r // 2, two(r), slots, :]
    step(1, 3)
    own_rows[1].last()

    @pl.loop(0, NX)
    def _(i):
        for j in range(NY):
            eb[i, j] = (gc[chip] * xc[1, x // 2, c, i, j, slots, :].astype(F32)).astype(BF)

    ex1 = exchange(1, lambda to: eb.at[to // 2, two(to)])
    ds[1, c, x, y, r] = eb[r // 2, two(r)]
    step(0, 2)
    for k in range(2):
        hidden = acc[0, k]
        tang = jnp.tanh(GELU_SCALE * (hidden + GELU_CUBIC * hidden * hidden * hidden))
        slope = 0.5 * (1.0 + tang) + 0.5 * hidden * (1.0 - tang * tang) * GELU_SCALE * (
            1.0 + 3.0 * GELU_CUBIC * hidden * hidden
        )
        acc[0, k] = slope
        zb[0, r, k] = (0.5 * hidden * (1.0 + tang)).astype(BF)
    zstep(0, 1)
    step(1, 1)
    for cp in ex0:
        cp.wait_recv()
    all_rows[0].first()
    step(1, 2)
    for k in range(2):
        zb[1, r, k] = (gate_col[k][:, 0:1] * acc[1, k] * acc[0, k]).astype(BF)
    zstep(1, 1)

    pair = []
    for k in range(2):

        @pl.loop(0, NX)
        def _(i):
            cols = pl.ds(pl.multiple_of(i * BLK, BLK), BLK)
            part = dot(zb[1, r, k], win[k, cols, :], 1, 1).astype(BF)
            for j in range(NY):
                for h in range(2):
                    ps[k, h, i, j] = part[:, (2 * j + h) * COL : (2 * j + h + 1) * COL]

        pair.append(send(ps.at[k, oc], rsib.at[k], sib))
        if k == 0:
            all_rows[0].second()
            zstep(0, 2)

    for k in range(2):
        gbuf[0, k] = lax.dot_general(
            jnp.ones((8, F), F32), zb[0, r, k].astype(F32) * acc[1, k], (((1,), (1,)), ((), ())),
            precision=lax.Precision.HIGHEST, preferred_element_type=F32,
        )
    g0 = send(gbuf.at[0], gsib, sib)

    stage1 = [[], []]
    for k in range(2):
        pair[k].wait_recv()

        @pl.loop(0, NX)
        def _(i):
            for j in range(NY):
                ps[k, c, i, j] = (ps[k, c, i, j].astype(F32) + rsib[k, i, j].astype(F32)).astype(BF)

        for d in (1, 3, 2):
            if k == 0:
                stage1[k].append(send(ps.at[0, c, xs(d)], rs1.at[0, x], dev(r, xs(d), y, c)))
            else:
                stage1[k].append(send(ps.at[1, c, :, ys(d)], rs1.at[1, y], dev(r, x, ys(d), c)))

    zstep(1, 2)
    for cp in ex1:
        cp.wait_recv()
    all_rows[1].first()
    all_rows[0].forward()

    g0.wait_recv()
    gbuf[1] = gbuf[0] + gsib[...]
    gx[x] = gbuf[1]
    g1 = [send(gbuf.at[1], gx.at[x], dev(r, xs(d), y, c)) for d in (1, 3, 2)]

    zstep(0, 3)
    all_rows[0].last()
    zstep(1, 3)

    stage2 = [[], []]
    for k in range(2):
        for cp in stage1[k]:
            cp.wait_recv()
        for j in range(4):
            total = (ps[0, c, x, j] if k == 0 else ps[1, c, j, y]).astype(F32)
            for d in (1, 2, 3):
                total += rs1[k, xs(d) if k == 0 else ys(d), j].astype(F32)
            ts[k, j] = total.astype(BF)
        for d in (1, 3, 2):
            if k == 0:
                stage2[k].append(send(ts.at[0, ys(d)], rs2.at[0, y], dev(r, x, ys(d), c)))
            else:
                stage2[k].append(send(ts.at[1, xs(d)], rs2.at[1, x], dev(r, xs(d), y, c)))

    all_rows[1].second()
    zstep(0, 4)
    for cp in g1:
        cp.wait_recv()
    gbuf[2] = (gx[0] + gx[1]) + (gx[2] + gx[3])
    gy[y] = gbuf[2]
    g2 = [send(gbuf.at[2], gy.at[y], dev(r, x, ys(d), c)) for d in (1, 3, 2)]

    expand = jnp.concatenate([hot(pos_row[k] == iota((PAD, CAP), 0)) for k in range(2)], axis=1)
    sums = []
    for k in range(2):
        for cp in stage2[k]:
            cp.wait_recv()
        total = ts[k, y if k == 0 else x].astype(F32)
        for d in (1, 2, 3):
            total += rs2[k, ys(d) if k == 0 else xs(d)].astype(F32)
        sums.append(total.astype(BF))
    ob[...] = dot(expand, jnp.concatenate(sums, axis=0)).astype(BF).reshape(2, NX, NY, ROWS, COL)

    back = plane(ob, rb, bsem, brsem)
    rb[c, x, y] = ob[c, x, y]
    zstep(1, 4)

    all_rows[1].forward()

    unpick = jnp.zeros((TOK, ROWS), F32)
    for k in range(2):
        bt = hot(ch_row[k] - e * TOK == iota((TOK, CAP), 0))
        at = hot(pos_col[k] - my_first == iota((CAP, ROWS), 1))
        unpick += dot(bt, at)
    unpick_ref[...] = unpick.astype(BF)

    for cp in g2:
        cp.wait_recv()
    total = (gy[0] + gy[1]) + (gy[2] + gy[3])
    for k in range(2):
        dgate_ref[0, k : k + 1, :] = total[k, 0:1, :]

    all_rows[1].last()

    def factor(w, k):
        return zb[w, :, k].reshape(NZ * CAP, F)

    def columns(a, k, j):
        blocks = [
            jnp.concatenate(
                [ds[a, h, 2 * k : 2 * k + 2, :, g, j].reshape(CAP, COL) for g in range(NZ)], axis=0
            )
            for h in range(2)
        ]
        return jnp.concatenate(blocks, axis=1)

    zstep(1, 5)
    all_rows[0].done()
    for k in range(2):
        for j in range(2):
            at = slice(j * 2 * COL, (j + 1) * 2 * COL)
            dwin_ref[k, at, :] = dot(columns(0, k, j), factor(1, k), 0, 0).astype(BF)
    zstep(0, 5)
    all_rows[1].done()
    for k in range(2):
        for j in range(2):
            at = slice(j * 2 * COL, (j + 1) * 2 * COL)
            dwout_ref[k, :, at] = dot(factor(0, k), columns(1, k, j), 0, 0).astype(BF)

    for cp in back:
        cp.wait_recv()
    rows_ref[...] = rb[...]

    assert counter[0] <= NSEM, counter[0]
    for cp in sent:
        cp.wait_send()

    for cp in forth + back:
        cp.wait_send()


def finish(rows_ref, unpick_ref, gate_ref, win_ref, wout_ref, dtok_ref, dgate_ref, dwin_ref, dwout_ref):
    for i in range(NX):
        rows = jnp.concatenate([rows_ref[h, i, j] for j in range(NY) for h in range(2)], axis=1)
        dtok_ref[0, :, i * BLK : (i + 1) * BLK] = dot(unpick_ref[...], rows).astype(BF)
    dgate_ref[...] = gate_ref[...]
    dwin_ref[...] = win_ref[...]
    dwout_ref[...] = wout_ref[...]


def local(tokens, grad_out, gates, chosen, w_in, w_out):
    hbm = pl.BlockSpec(memory_space=pl.ANY)
    vmem = pl.BlockSpec(memory_space=pltpu.VMEM)
    dma = pltpu.SemaphoreType.DMA
    d_gate = jax.ShapeDtypeStruct((1, 2, CAP), F32)
    d_in = jax.ShapeDtypeStruct((2, D // NZ, F), BF)
    d_out = jax.ShapeDtypeStruct((2, F, D // NZ), BF)
    parts = pl.pallas_call(
        kernel,
        out_shape=(
            jax.ShapeDtypeStruct((2, NX, NY, ROWS, COL), BF),
            jax.ShapeDtypeStruct((TOK, ROWS), BF),
            d_gate,
            d_in,
            d_out,
        ),
        in_specs=[hbm, hbm, vmem, vmem, hbm, hbm],
        out_specs=(vmem,) * 5,
        scratch_shapes=[
            pltpu.VMEM((TOK, D), BF),
            pltpu.VMEM((TOK, D), BF),
            pltpu.VMEM((2, D, F), BF),
            pltpu.VMEM((2, F, D), BF),
            pltpu.VMEM((2, NX, NY, 2, ROWS, COL), BF),
            pltpu.VMEM((2, NX, NY, 2, ROWS, COL), BF),
            pltpu.VMEM((2, 2, 2, NX, NY, CAP, COL), BF),
            pltpu.VMEM((NX * NY, ROWS, COL), F32),
            pltpu.VMEM((NX, NY, ROWS, COL), BF),
            pltpu.VMEM((2, 2, NX, NY, NZ, 2, ROWS, COL), BF),
            pltpu.VMEM((2, NZ, 2, CAP, F), BF),
            pltpu.VMEM((2, 2, CAP, F), F32),
            pltpu.VMEM((2, 2, NX, NY, CAP, COL), BF),
            pltpu.VMEM((2, NX, NY, CAP, COL), BF),
            pltpu.VMEM((2, 4, 4, CAP, COL), BF),
            pltpu.VMEM((2, 4, CAP, COL), BF),
            pltpu.VMEM((2, 4, CAP, COL), BF),
            pltpu.VMEM((2, NX, NY, ROWS, COL), BF),
            pltpu.VMEM((2, NX, NY, ROWS, COL), BF),
            pltpu.VMEM((3, 2, 8, CAP), F32),
            pltpu.VMEM((2, 8, CAP), F32),
            pltpu.VMEM((4, 2, 8, CAP), F32),
            pltpu.VMEM((4, 2, 8, CAP), F32),
            dma((NSEM,)),
            dma((NSEM,)),
            dma((PLANE,)),
            dma((PLANE,)),
            dma((PLANE,)),
            dma((PLANE,)),
            dma((4,)),
        ],
        compiler_params=pltpu.CompilerParams(
            collective_id=0, has_side_effects=True, vmem_limit_bytes=60 << 20
        ),
        name="expert_backward",
    )(tokens, grad_out, gates, chosen, w_in, w_out)
    return pl.pallas_call(
        finish,
        out_shape=(jax.ShapeDtypeStruct((1, TOK, D), BF), d_gate, d_in, d_out),
        in_specs=[vmem] * 5,
        out_specs=(vmem,) * 4,
        compiler_params=pltpu.CompilerParams(vmem_limit_bytes=60 << 20),
        name="finish",
    )(*parts)


def solution(mesh):
    return jax.shard_map(
        local,
        mesh=mesh,
        in_specs=(
            P("rep", "exp", None),
            P("rep", "exp", None),
            P("rep", None, None),
            P("rep", None, None),
            P(None, None, "exp"),
            P(None, "exp", None),
        ),
        out_specs=(
            P("rep", "exp", None),
            P("rep", None, None),
            P(None, "rep", "exp"),
            P(None, "exp", "rep"),
        ),
        check_vma=False,
    )
```

```python
import jax
import jax.numpy as jnp
from jax import lax
from jax.experimental import pallas as pl
from jax.experimental.pallas import tpu as pltpu
from jax.sharding import PartitionSpec as P

GELU_SCALE = 0.7978845608028654
GELU_CUBIC = 0.044715

BF = jnp.bfloat16
F32 = jnp.float32
MESH = pl.DeviceIdType.MESH

NX, NY, NZ = 4, 4, 8
D = 4096
F = 256
CAP = 128
TOK = 128
MOST = 8
ROWS = 2 * MOST
PAD = NX * NY * 2 * ROWS
COL = 128
BLK = D // NX
PLANE = NX * NY * 2

NSEM = 144

ORDER = (
    ("slot", 0), ("cols", 0, 2), ("ring", 0, 2), ("slot", 1), ("cols", 1, 1), ("gate", 0), ("pair", 0), ("pair", 1), ("ring", 1, 2), ("cols", 0, 3), ("cols", 1, 2), ("gate", 1), ("ring", 0, 3), ("ring", 1, 3), ("sum", 0), ("sum", 1), ("ring", 0, 4), ("cols", 0, 4), ("gate", 2), ("ring", 1, 4), ("cols", 1, 3), ("back",), ("pick",), ("gate", 3), ("cols", 1, 4),
)


def dot(a, b, ca=1, cb=0):
    return lax.dot_general(a, b, (((ca,), (cb,)), ((), ())), preferred_element_type=F32)


def kernel(
    tok_hbm, grad_hbm, gates_ref, chosen_ref, win_hbm, wout_hbm,
    rows_hbm, unpick_hbm, dgate_hbm, dwin_hbm, dwout_hbm,
    unpick_ref, dgate_ref, dwin_ref, dwout_ref, tok, grad, win, wout, pk, rp, xc, gc, eb, ds, zb, acc, ps, rsib, rs1, ts, rs2, ob, rb,
    gbuf, gsib, gx, gy,
    ssem, rsem, asem, arsem, bsem, brsem, lsem, osem,
):
    r = lax.axis_index("rep")
    e = lax.axis_index("exp")
    x = e // 8
    y = (e // 2) % 4
    c = e % 2
    oc = 1 - c
    chip = x * NY + y

    def dev(rr, xx, yy, c_):
        return (rr, (xx * 4 + yy) * 2 + c_)

    def xs(d):
        return lax.rem(x + d, 4)

    def ys(d):
        return lax.rem(y + d, 4)

    def zs(d):
        return lax.rem(r + d, 8)

    sib = dev(r, x, y, oc)

    loads = [
        pltpu.make_async_copy(tok_hbm.at[0], tok, lsem.at[0]),
        pltpu.make_async_copy(grad_hbm.at[0], grad, lsem.at[1]),
        pltpu.make_async_copy(win_hbm, win, lsem.at[2]),
        pltpu.make_async_copy(wout_hbm, wout, lsem.at[3]),
    ]
    loads[0].start()
    loads[1].start()

    barrier = pltpu.get_barrier_semaphore()

    for i in range(1, PLANE):
        to = dev(r, xs(i // 8), ys((i // 2) % 4), oc if i % 2 else c)
        pl.semaphore_signal(barrier, inc=1, device_id=to, device_id_type=MESH)
    for d in range(1, NZ):
        pl.semaphore_signal(barrier, inc=1, device_id=dev(zs(d), x, y, c), device_id_type=MESH)

    counter = [0]
    sent = []

    def send(src, dst, to):
        i = counter[0]
        counter[0] += 1
        cp = pltpu.make_async_remote_copy(
            src_ref=src, dst_ref=dst, send_sem=ssem.at[i], recv_sem=rsem.at[i],
            device_id=to, device_id_type=MESH,
        )
        cp.start()
        sent.append(cp)
        return cp

    def iota(shape, dim):
        return lax.broadcasted_iota(jnp.int32, shape, dim)

    def hot(m):
        return jnp.where(m, 1.0, 0.0).astype(BF)

    sq = (CAP, CAP)
    my_first = (c * (NX * NY) + chip) * ROWS
    ch_row, ch_col, pos_row, pos_col, gate_col = [], [], [], [], []
    for k in range(2):
        row = chosen_ref[0, k : k + 1, :]
        rb_ = jnp.broadcast_to(row, sq)
        cb_ = rb_.T
        same = (rb_ // TOK) == (cb_ // TOK)
        rank_col = jnp.sum(jnp.where(same & (iota(sq, 1) < iota(sq, 0)), 1, 0), axis=1, keepdims=True)
        rank_row = jnp.sum(jnp.where(same & (iota(sq, 0) < iota(sq, 1)), 1, 0), axis=0, keepdims=True)

        def place(own, rank):
            return ((own % 2) * (NX * NY) + own // 2) * ROWS + k * MOST + rank

        ch_row.append(row)
        ch_col.append(cb_[:, 0:1])
        pos_row.append(place(row // TOK, rank_row))
        pos_col.append(place(cb_[:, 0:1] // TOK, rank_col))

    pick = jnp.zeros((ROWS, TOK), F32)
    for k in range(2):
        a = hot(pos_row[k] - my_first == iota((ROWS, CAP), 0))
        b = hot(ch_col[k] - e * TOK == iota((CAP, TOK), 1))
        pick += dot(a, b)
    pick = pick.astype(BF)

    loads[0].wait()
    loads[1].wait()
    loads[2].start()
    loads[3].start()

    @pl.loop(0, NX)
    def _(i):
        cols = pl.ds(pl.multiple_of(i * BLK, BLK), BLK)
        xr = dot(pick, tok[:, cols]).astype(BF)
        dr = dot(pick, grad[:, cols]).astype(BF)
        for j in range(NY):
            for k in range(2):
                at = slice((2 * j + k) * COL, (2 * j + k + 1) * COL)
                pk[k, i, j, 0] = xr[:, at]
                pk[k, i, j, 1] = dr[:, at]

    pl.semaphore_wait(barrier, PLANE - 1 + NZ - 1)

    def plane(src, dst, s_sem, r_sem):
        copies = []
        for i in range(1, PLANE):
            px, py, pc = xs(i // 8), ys((i // 2) % 4), (oc if i % 2 else c)
            cp = pltpu.make_async_remote_copy(
                src_ref=src.at[pc, px, py], dst_ref=dst.at[c, x, y], send_sem=s_sem.at[i],
                recv_sem=r_sem.at[i], device_id=dev(r, px, py, pc), device_id_type=MESH,
            )
            cp.start()
            copies.append(cp)
        return copies

    forth = plane(pk, rp, asem, arsem)
    rp[c, x, y] = pk[c, x, y]
    gather = jnp.concatenate([hot(pos_col[k] == iota((CAP, PAD), 1)) for k in range(2)], axis=0)
    for k in range(2):
        gate_col.append(jnp.broadcast_to(gates_ref[0, k : k + 1, :], sq).T)
        gc[k * 8 : (k + 1) * 8] = gate_col[k].reshape(8, ROWS, COL)

    for cp in forth:
        cp.wait_recv()

    both = jnp.concatenate([rp[:, :, :, k].reshape(PAD, COL) for k in range(2)], axis=1)
    both = dot(gather, both).astype(BF)
    for a in range(2):
        for k in range(2):
            xc[a, k, c, x, y] = both[k * CAP : (k + 1) * CAP, a * COL : (a + 1) * COL]

    class Spread:
        def __init__(self, row):
            self.row = row

        def block(self, k):
            return self.row(k, 0, x if k == 0 else y)

        def first(self):
            self.got = []
            for d in (1, 3, 2):
                for k, to in ((0, dev(r, xs(d), y, c)), (1, dev(r, x, ys(d), c))):
                    ref = self.block(k)
                    self.got.append(send(ref, ref, to))

        def along(self, k, d):
            return dev(r, x, ys(d), c) if k == 0 else dev(r, xs(d), y, c)

        def second(self):
            for cp in self.got:
                cp.wait_recv()
            self.got = []
            for k in range(2):
                ref = self.row(k, 0, slice(0, 4))
                for d in (1, 3):
                    self.got.append(send(ref, ref, self.along(k, d)))
            self.sibs = {}
            self.share(0)

        def forward(self):
            got, self.got = self.got, []
            for k in range(2):
                for n, (d, at) in enumerate(((3, slice(0, 2)), (1, slice(2, 4)))):
                    got[2 * k + n].wait_recv()
                    ref = self.row(k, d, at)
                    self.got.append(send(ref, ref, self.along(k, 1 if d == 3 else 3)))
            self.share(3)
            self.share(1)

        def share(self, d):
            refs = [self.row(k, d, slice(0, 4)) for k in range(2)]
            self.sibs[d] = [send(ref, ref, sib) for ref in refs]

        def last(self):
            for cp in self.got:
                cp.wait_recv()
            self.share(2)

        def done(self, rows=(0, 3, 1, 2)):
            for d in rows:
                for cp in self.sibs[d]:
                    cp.wait_recv()

    def rows_of(a):
        return lambda k, d, at: xc.at[a, 0, c, at, ys(d)] if k == 0 else xc.at[a, 1, c, xs(d), at]

    def columns_of(a):
        return lambda k, d, at: ds.at[a, c, at, ys(d), 0:4] if k == 0 else ds.at[a, c, xs(d), at, 4:8]

    own_rows = [Spread(rows_of(a)) for a in range(2)]
    all_rows = [Spread(columns_of(a)) for a in range(2)]
    slots = pl.ds(pl.multiple_of(lax.rem(chip, 8) * ROWS, ROWS), ROWS)

    def two(to):
        return pl.ds(2 * lax.rem(to, 2), 2)

    def exchange(a, src):
        copies = []
        for d in (1, 7, 2, 6, 3, 5, 4):
            copies.append(send(src(zs(d)), ds.at[a, c, x, y, r], dev(zs(d), x, y, c)))
        return copies

    right, left = dev(zs(1), x, y, c), dev(zs(7), x, y, c)
    ring = [None, None]

    def zstep(w, s):
        if s > 1:
            for cp in ring[w]:
                cp.wait_recv()
        if s < 4:
            ra, la = zb.at[w, zs(9 - s)], zb.at[w, zs(s - 1)]
        elif s == 4:
            ra, la = zb.at[w, zs(5), 0], zb.at[w, zs(3), 1]
        else:
            return
        ring[w] = [send(ra, ra, right), send(la, la, left)]

    def step(a, d):
        own_rows[a].done((d,))
        for k in range(2):
            total = None
            for j in range(4):
                px, py = (j, ys(d)) if k == 0 else (xs(d), j)
                lhs = jnp.concatenate([xc[a, k, h, px, py] for h in range(2)], axis=1)
                cols = pl.ds(pl.multiple_of((px * NY + py) * 2 * COL, 2 * COL), 2 * COL)
                part = dot(lhs, win[k, cols, :]) if a == 0 else dot(lhs, wout[k, :, cols], 1, 1)
                total = part if total is None else total + part
            acc[a, k] = total if d == 0 else acc[a, k] + total

    for sp in own_rows:
        sp.first()
    for sp in own_rows:
        sp.second()
    loads[2].wait()
    loads[3].wait()
    step(0, 0)
    own_rows[0].forward()
    step(1, 0)
    own_rows[1].forward()
    step(0, 3)
    step(0, 1)
    own_rows[0].last()
    ex0 = exchange(0, lambda to: xc.at[0, x // 2, c, to // 2, two(to), slots])
    ds[0, c, x, y, r] = xc[0, x // 2, c, r // 2, two(r), slots, :]
    step(1, 3)
    step(0, 2)
    own_rows[1].last()
    for k in range(2):
        hidden = acc[0, k]
        tang = jnp.tanh(GELU_SCALE * (hidden + GELU_CUBIC * hidden * hidden * hidden))
        slope = 0.5 * (1.0 + tang) + 0.5 * hidden * (1.0 - tang * tang) * GELU_SCALE * (
            1.0 + 3.0 * GELU_CUBIC * hidden * hidden
        )
        acc[0, k] = slope
        zb[0, r, k] = (0.5 * hidden * (1.0 + tang)).astype(BF)
    zstep(0, 1)
    step(1, 1)

    @pl.loop(0, NX)
    def _(i):
        for j in range(NY):
            eb[i, j] = (gc[chip] * xc[1, x // 2, c, i, j, slots, :].astype(F32)).astype(BF)

    ex1 = exchange(1, lambda to: eb.at[to // 2, two(to)])
    ds[1, c, x, y, r] = eb[r // 2, two(r)]
    for cp in ex0:
        cp.wait_recv()
    all_rows[0].first()
    step(1, 2)
    for k in range(2):
        zb[1, r, k] = (gate_col[k][:, 0:1] * acc[1, k] * acc[0, k]).astype(BF)
    zstep(1, 1)
    pair, stage1, stage2, gates_on_way, kept = {}, {0: [], 1: []}, {0: [], 1: []}, {}, {}
    outs = []

    def leave(src, dst):
        cp = pltpu.make_async_copy(src, dst, osem.at[len(outs)])
        cp.start()
        outs.append(cp)

    def slot_part(k):
        @pl.loop(0, NX)
        def _(i):
            cols = pl.ds(pl.multiple_of(i * BLK, BLK), BLK)
            part = dot(win[k, cols, :], zb[1, r, k], 1, 1).astype(BF)
            for j in range(NY):
                for h in range(2):
                    ps[k, h, i, j] = part[(2 * j + h) * COL : (2 * j + h + 1) * COL]

        pair[k] = send(ps.at[k, oc], rsib.at[k], sib)

    def pair_sum(k):
        pair[k].wait_recv()

        @pl.loop(0, NX)
        def _(i):
            for j in range(NY):
                ps[k, c, i, j] = (ps[k, c, i, j].astype(F32) + rsib[k, i, j].astype(F32)).astype(BF)

        for d in (1, 3, 2):
            if k == 0:
                stage1[k].append(send(ps.at[0, c, xs(d)], rs1.at[0, x], dev(r, xs(d), y, c)))
            else:
                stage1[k].append(send(ps.at[1, c, :, ys(d)], rs1.at[1, y], dev(r, x, ys(d), c)))

    def first_sum(k):
        for cp in stage1[k]:
            cp.wait_recv()
        for j in range(4):
            total = (ps[0, c, x, j] if k == 0 else ps[1, c, j, y]).astype(F32)
            for d in (1, 2, 3):
                total += rs1[k, xs(d) if k == 0 else ys(d), j].astype(F32)
            ts[k, j] = total.astype(BF)
        for d in (1, 3, 2):
            if k == 0:
                stage2[k].append(send(ts.at[0, ys(d)], rs2.at[0, y], dev(r, x, ys(d), c)))
            else:
                stage2[k].append(send(ts.at[1, xs(d)], rs2.at[1, x], dev(r, xs(d), y, c)))

    def return_rows():
        expand = jnp.concatenate([hot(pos_row[k] == iota((PAD, CAP), 0)) for k in range(2)], axis=1)
        sums = []
        for k in range(2):
            for cp in stage2[k]:
                cp.wait_recv()
            total = ts[k, y if k == 0 else x].astype(F32)
            for d in (1, 2, 3):
                total += rs2[k, ys(d) if k == 0 else xs(d)].astype(F32)
            sums.append(total.astype(BF))
        sums = jnp.concatenate(sums, axis=1)
        ob[...] = dot(expand, sums, 1, 1).astype(BF).reshape(2, NX, NY, ROWS, COL)
        kept["back"] = plane(ob, rb, bsem, brsem)
        rb[c, x, y] = ob[c, x, y]

    def gate_sum(n):
        if n == 0:
            for k in range(2):
                gbuf[0, k] = lax.dot_general(
                    jnp.ones((8, F), F32), zb[0, r, k].astype(F32) * acc[1, k], (((1,), (1,)), ((), ())),
                    precision=lax.Precision.HIGHEST, preferred_element_type=F32,
                )
            gates_on_way[0] = [send(gbuf.at[0], gsib, sib)]
            return
        for cp in gates_on_way[n - 1]:
            cp.wait_recv()
        if n == 1:
            gbuf[1] = gbuf[0] + gsib[...]
            gx[x] = gbuf[1]
            gates_on_way[1] = [send(gbuf.at[1], gx.at[x], dev(r, xs(d), y, c)) for d in (1, 3, 2)]
        elif n == 2:
            gbuf[2] = (gx[0] + gx[1]) + (gx[2] + gx[3])
            gy[y] = gbuf[2]
            gates_on_way[2] = [send(gbuf.at[2], gy.at[y], dev(r, x, ys(d), c)) for d in (1, 3, 2)]
        else:
            total = (gy[0] + gy[1]) + (gy[2] + gy[3])
            for k in range(2):
                dgate_ref[0, k : k + 1, :] = total[k, 0:1, :]
            leave(dgate_ref, dgate_hbm)

    def column_spread(a, n):
        sp = all_rows[a]
        if n == 1:
            if a == 1:
                for cp in ex1:
                    cp.wait_recv()
            sp.first()
        else:
            (None, None, sp.second, sp.forward, sp.last)[n]()

    def owner_pick():
        unpick = jnp.zeros((TOK, ROWS), F32)
        for k in range(2):
            bt = hot(ch_row[k] - e * TOK == iota((TOK, CAP), 0))
            at = hot(pos_col[k] - my_first == iota((CAP, ROWS), 1))
            unpick += dot(bt, at)
        unpick_ref[...] = unpick.astype(BF)
        leave(unpick_ref, unpick_hbm)

    steps = {
        "slot": slot_part, "pair": pair_sum, "sum": first_sum, "back": return_rows, "gate": gate_sum,
        "ring": zstep, "cols": column_spread, "pick": owner_pick,
    }
    for name, *at in ORDER:
        steps[name](*at)

    def factor(w, k):
        return zb[w, :, k].reshape(NZ * CAP, F)

    def columns(a, k, j):
        blocks = [
            jnp.concatenate(
                [ds[a, h, 2 * k : 2 * k + 2, :, g, j].reshape(CAP, COL) for g in range(NZ)], axis=0
            )
            for h in range(2)
        ]
        return jnp.concatenate(blocks, axis=1)

    zstep(1, 5)
    all_rows[0].done()
    for k in range(2):
        for j in range(2):
            at = slice(j * 2 * COL, (j + 1) * 2 * COL)
            dwin_ref[k, at, :] = dot(columns(0, k, j), factor(1, k), 0, 0).astype(BF)
    leave(dwin_ref, dwin_hbm)
    zstep(0, 5)
    all_rows[1].done()
    for k in range(2):
        for j in range(2):
            at = slice(j * 2 * COL, (j + 1) * 2 * COL)
            dwout_ref[k, :, at] = dot(factor(0, k), columns(1, k, j), 0, 0).astype(BF)
    leave(dwout_ref, dwout_hbm)

    for cp in kept["back"]:
        cp.wait_recv()
    leave(rb, rows_hbm)

    assert counter[0] <= NSEM, counter[0]
    for cp in sent:
        cp.wait_send()

    for cp in forth + kept["back"]:
        cp.wait_send()
    for cp in outs:
        cp.wait()


def finish(
    rows_hbm, unpick_hbm, gate_hbm, win_hbm, wout_hbm, dtok_hbm, dgate_hbm, dwin_hbm, dwout_hbm,
    rows, unpick, gate, win, wout, dtok, isem, osem,
):
    ins = [
        pltpu.make_async_copy(src, dst, isem.at[i])
        for i, (src, dst) in enumerate(
            ((rows_hbm, rows), (unpick_hbm, unpick), (gate_hbm, gate), (win_hbm, win), (wout_hbm, wout))
        )
    ]
    for cp in ins:
        cp.start()
    outs = []

    def leave(src, dst):
        cp = pltpu.make_async_copy(src, dst, osem.at[len(outs)])
        cp.start()
        outs.append(cp)

    ins[0].wait()
    ins[1].wait()
    for i in range(NX):
        block = jnp.concatenate([rows[h, i, j] for j in range(NY) for h in range(2)], axis=1)
        at = pl.ds(i * BLK, BLK)
        dtok[0, :, at] = dot(unpick[...], block).astype(BF)
        leave(dtok.at[0, :, at], dtok_hbm.at[0, :, at])
    for cp, src, dst in zip(ins[2:], (gate, win, wout), (dgate_hbm, dwin_hbm, dwout_hbm)):
        cp.wait()
        leave(src, dst)
    for cp in outs:
        cp.wait()


def local(tokens, grad_out, gates, chosen, w_in, w_out):
    hbm = pl.BlockSpec(memory_space=pl.ANY)
    vmem = pl.BlockSpec(memory_space=pltpu.VMEM)
    dma = pltpu.SemaphoreType.DMA
    d_gate = jax.ShapeDtypeStruct((1, 2, CAP), F32)
    d_in = jax.ShapeDtypeStruct((2, D // NZ, F), BF)
    d_out = jax.ShapeDtypeStruct((2, F, D // NZ), BF)
    parts = pl.pallas_call(
        kernel,
        out_shape=(
            jax.ShapeDtypeStruct((2, NX, NY, ROWS, COL), BF),
            jax.ShapeDtypeStruct((TOK, ROWS), BF),
            d_gate,
            d_in,
            d_out,
        ),
        in_specs=[hbm, hbm, vmem, vmem, hbm, hbm],
        out_specs=(hbm,) * 5,
        scratch_shapes=[
            pltpu.VMEM((TOK, ROWS), BF),
            pltpu.VMEM((1, 2, CAP), F32),
            pltpu.VMEM((2, D // NZ, F), BF),
            pltpu.VMEM((2, F, D // NZ), BF),
            pltpu.VMEM((TOK, D), BF),
            pltpu.VMEM((TOK, D), BF),
            pltpu.VMEM((2, D, F), BF),
            pltpu.VMEM((2, F, D), BF),
            pltpu.VMEM((2, NX, NY, 2, ROWS, COL), BF),
            pltpu.VMEM((2, NX, NY, 2, ROWS, COL), BF),
            pltpu.VMEM((2, 2, 2, NX, NY, CAP, COL), BF),
            pltpu.VMEM((NX * NY, ROWS, COL), F32),
            pltpu.VMEM((NX, NY, ROWS, COL), BF),
            pltpu.VMEM((2, 2, NX, NY, NZ, 2, ROWS, COL), BF),
            pltpu.VMEM((2, NZ, 2, CAP, F), BF),
            pltpu.VMEM((2, 2, CAP, F), F32),
            pltpu.VMEM((2, 2, NX, NY, CAP, COL), BF),
            pltpu.VMEM((2, NX, NY, CAP, COL), BF),
            pltpu.VMEM((2, 4, 4, CAP, COL), BF),
            pltpu.VMEM((2, 4, CAP, COL), BF),
            pltpu.VMEM((2, 4, CAP, COL), BF),
            pltpu.VMEM((2, NX, NY, ROWS, COL), BF),
            pltpu.VMEM((2, NX, NY, ROWS, COL), BF),
            pltpu.VMEM((3, 2, 8, CAP), F32),
            pltpu.VMEM((2, 8, CAP), F32),
            pltpu.VMEM((4, 2, 8, CAP), F32),
            pltpu.VMEM((4, 2, 8, CAP), F32),
            dma((NSEM,)),
            dma((NSEM,)),
            dma((PLANE,)),
            dma((PLANE,)),
            dma((PLANE,)),
            dma((PLANE,)),
            dma((4,)),
            dma((5,)),
        ],
        compiler_params=pltpu.CompilerParams(
            collective_id=0, has_side_effects=True, vmem_limit_bytes=60 << 20
        ),
        name="expert_backward",
    )(tokens, grad_out, gates, chosen, w_in, w_out)
    return pl.pallas_call(
        finish,
        out_shape=(jax.ShapeDtypeStruct((1, TOK, D), BF), d_gate, d_in, d_out),
        in_specs=[hbm] * 5,
        out_specs=(hbm,) * 4,
        scratch_shapes=[
            pltpu.VMEM((2, NX, NY, ROWS, COL), BF),
            pltpu.VMEM((TOK, ROWS), BF),
            pltpu.VMEM((1, 2, CAP), F32),
            pltpu.VMEM((2, D // NZ, F), BF),
            pltpu.VMEM((2, F, D // NZ), BF),
            pltpu.VMEM((1, TOK, D), BF),
            dma((5,)),
            dma((7,)),
        ],
        compiler_params=pltpu.CompilerParams(vmem_limit_bytes=60 << 20),
        name="finish",
    )(*parts)


def solution(mesh):
    return jax.shard_map(
        local,
        mesh=mesh,
        in_specs=(
            P("rep", "exp", None),
            P("rep", "exp", None),
            P("rep", None, None),
            P("rep", None, None),
            P(None, None, "exp"),
            P(None, "exp", None),
        ),
        out_specs=(
            P("rep", "exp", None),
            P("rep", None, None),
            P(None, "rep", "exp"),
            P(None, "exp", "rep"),
        ),
        check_vma=False,
    )
```

```python
import jax
import jax.numpy as jnp
from jax import lax
from jax.experimental import pallas as pl
from jax.experimental.pallas import tpu as pltpu
from jax.sharding import PartitionSpec as P

GELU_SCALE = 0.7978845608028654
GELU_CUBIC = 0.044715

BF = jnp.bfloat16
F32 = jnp.float32
MESH = pl.DeviceIdType.MESH

NX, NY, NZ = 4, 4, 8
D = 4096
F = 256
CAP = 128
TOK = 128
MOST = 8
ROWS = 2 * MOST
PAD = NX * NY * 2 * ROWS
COL = 128
BLK = D // NX
PLANE = NX * NY * 2

NSEM = 144

ORDER = (
    ("cols", 2), ("slot", 0), ("ring", 0, 2), ("slot", 1), ("gate", 0), ("pair", 0), ("pair", 1), ("ring", 1, 2), ("cols", 3), ("gate", 1), ("ring", 0, 3), ("ring", 1, 3), ("sum", 0), ("sum", 1), ("ring", 0, 4), ("gate", 2), ("ring", 1, 4), ("cols", 4), ("back",), ("pick",), ("gate", 3),
)


def dot(a, b, ca=1, cb=0):
    return lax.dot_general(a, b, (((ca,), (cb,)), ((), ())), preferred_element_type=F32)


def kernel(
    tok_hbm, grad_hbm, gates_ref, chosen_ref, win_hbm, wout_hbm,
    rows_hbm, unpick_hbm, dgate_hbm, dwin_hbm, dwout_hbm,
    unpick_ref, dgate_ref, dwin_ref, dwout_ref, tok, grad, win, wout, pk, rp, xc, cross_out, xd, zb, acc, ps, rsib, rs1, ts, rs2, ob, rb, rows_out,
    gbuf, gsib, gx, gy,
    ssem, rsem, asem, arsem, bsem, brsem, lsem, osem, csem,
):
    r = lax.axis_index("rep")
    e = lax.axis_index("exp")
    x = e // 8
    y = (e // 2) % 4
    c = e % 2
    oc = 1 - c
    chip = x * NY + y

    def dev(rr, xx, yy, c_):
        return (rr, (xx * 4 + yy) * 2 + c_)

    def xs(d):
        return lax.rem(x + d, 4)

    def ys(d):
        return lax.rem(y + d, 4)

    def zs(d):
        return lax.rem(r + d, 8)

    sib = dev(r, x, y, oc)

    loads = [
        pltpu.make_async_copy(tok_hbm.at[0], tok, lsem.at[0]),
        pltpu.make_async_copy(grad_hbm.at[0], grad, lsem.at[1]),
        pltpu.make_async_copy(win_hbm, win, lsem.at[2]),
        pltpu.make_async_copy(wout_hbm, wout, lsem.at[3]),
    ]
    loads[0].start()
    loads[1].start()

    barrier = pltpu.get_barrier_semaphore()

    for i in range(1, PLANE):
        to = dev(r, xs(i // 8), ys((i // 2) % 4), oc if i % 2 else c)
        pl.semaphore_signal(barrier, inc=1, device_id=to, device_id_type=MESH)
    for d in range(1, NZ):
        pl.semaphore_signal(barrier, inc=1, device_id=dev(zs(d), x, y, c), device_id_type=MESH)

    m = e // 4
    away = m != 0

    def turned(p):
        return lax.rem(p + 2 * r, NX * NY)
    counter = [0]
    sent = []

    def send(src, dst, to):
        i = counter[0]
        counter[0] += 1
        cp = pltpu.make_async_remote_copy(
            src_ref=src, dst_ref=dst, send_sem=ssem.at[i], recv_sem=rsem.at[i],
            device_id=to, device_id_type=MESH,
        )
        cp.start()
        sent.append(cp)
        return cp

    def iota(shape, dim):
        return lax.broadcasted_iota(jnp.int32, shape, dim)

    def hot(m):
        return jnp.where(m, 1.0, 0.0).astype(BF)

    sq = (CAP, CAP)
    my_first = (c * (NX * NY) + chip) * ROWS
    ch_row, ch_col, pos_row, pos_col, gate_col = [], [], [], [], []
    for k in range(2):
        row = chosen_ref[0, k : k + 1, :]
        rb_ = jnp.broadcast_to(row, sq)
        cb_ = rb_.T
        same = (rb_ // TOK) == (cb_ // TOK)
        rank_col = jnp.sum(jnp.where(same & (iota(sq, 1) < iota(sq, 0)), 1, 0), axis=1, keepdims=True)
        rank_row = jnp.sum(jnp.where(same & (iota(sq, 0) < iota(sq, 1)), 1, 0), axis=0, keepdims=True)

        def place(own, rank):
            return ((own % 2) * (NX * NY) + own // 2) * ROWS + k * MOST + rank

        ch_row.append(row)
        ch_col.append(cb_[:, 0:1])
        pos_row.append(place(row // TOK, rank_row))
        pos_col.append(place(cb_[:, 0:1] // TOK, rank_col))

    pick = jnp.zeros((ROWS, TOK), F32)
    for k in range(2):
        a = hot(pos_row[k] - my_first == iota((ROWS, CAP), 0))
        b = hot(ch_col[k] - e * TOK == iota((CAP, TOK), 1))
        pick += dot(a, b)
    pick = pick.astype(BF)

    loads[0].wait()
    loads[1].wait()
    loads[2].start()
    loads[3].start()

    def wide(p):
        return pl.ds(pl.multiple_of(turned(p) * 2 * COL, 2 * COL), 2 * COL)

    @pl.loop(0, NX)
    def _(i):
        for j in range(NY):
            cols = wide(i * NY + j)
            xr = dot(pick, tok[:, cols]).astype(BF)
            dr = dot(pick, grad[:, cols]).astype(BF)
            for k in range(2):
                pk[k, i, j, 0] = xr[:, k * COL : (k + 1) * COL]
                pk[k, i, j, 1] = dr[:, k * COL : (k + 1) * COL]

    pl.semaphore_wait(barrier, PLANE - 1 + NZ - 1)


    def plane(src, dst, s_sem, r_sem):
        copies = []
        for i in range(1, PLANE):
            px, py, pc = xs(i // 8), ys((i // 2) % 4), (oc if i % 2 else c)
            cp = pltpu.make_async_remote_copy(
                src_ref=src.at[pc, px, py], dst_ref=dst.at[c, x, y], send_sem=s_sem.at[i],
                recv_sem=r_sem.at[i], device_id=dev(r, px, py, pc), device_id_type=MESH,
            )
            cp.start()
            copies.append(cp)
        return copies

    forth = plane(pk, rp, asem, arsem)
    rp[c, x, y] = pk[c, x, y]
    gather = jnp.concatenate([hot(pos_col[k] == iota((CAP, PAD), 1)) for k in range(2)], axis=0)
    for k in range(2):
        gate_col.append(jnp.broadcast_to(gates_ref[0, k : k + 1, :], sq).T)

    for cp in forth:
        cp.wait_recv()

    both = jnp.concatenate([rp[:, :, :, k].reshape(PAD, COL) for k in range(2)], axis=1)
    both = dot(gather, both)
    for a in range(2):
        for k in range(2):
            block = both[k * CAP : (k + 1) * CAP, a * COL : (a + 1) * COL]
            xc[a, k, c, x, y] = block.astype(BF)
            cross_out[k, a] = (block if a == 0 else gate_col[k] * block).astype(BF)

    class Spread:
        def __init__(self, row):
            self.row = row

        def block(self, k):
            return self.row(k, 0, x if k == 0 else y)

        def first(self):
            self.got = []
            for d in (1, 3, 2):
                for k, to in ((0, dev(r, xs(d), y, c)), (1, dev(r, x, ys(d), c))):
                    ref = self.block(k)
                    self.got.append(send(ref, ref, to))

        def along(self, k, d):
            return dev(r, x, ys(d), c) if k == 0 else dev(r, xs(d), y, c)

        def second(self):
            for cp in self.got:
                cp.wait_recv()
            self.got = []
            for k in range(2):
                ref = self.row(k, 0, slice(0, 4))
                for d in (1, 3):
                    self.got.append(send(ref, ref, self.along(k, d)))
            self.sibs = {}
            self.share(0)

        def forward(self):
            got, self.got = self.got, []
            for k in range(2):
                for n, (d, at) in enumerate(((3, slice(0, 2)), (1, slice(2, 4)))):
                    got[2 * k + n].wait_recv()
                    ref = self.row(k, d, at)
                    self.got.append(send(ref, ref, self.along(k, 1 if d == 3 else 3)))
            self.share(3)
            self.share(1)

        def share(self, d):
            refs = [self.row(k, d, slice(0, 4)) for k in range(2)]
            self.sibs[d] = [send(ref, ref, sib) for ref in refs]

        def last(self):
            for cp in self.got:
                cp.wait_recv()
            self.share(2)

        def done(self, rows=(0, 3, 1, 2)):
            for d in rows:
                for cp in self.sibs[d]:
                    cp.wait_recv()

    def rows_of(a):
        return lambda k, d, at: xc.at[a, 0, c, at, ys(d)] if k == 0 else xc.at[a, 1, c, xs(d), at]

    def columns(k, d, at):
        return xd.at[0, c, at, ys(d)] if k == 0 else xd.at[1, c, xs(d), at]

    own_rows = [Spread(rows_of(a)) for a in range(2)]
    all_rows = Spread(columns)

    cross = pltpu.make_async_remote_copy(
        src_ref=cross_out, dst_ref=xd.at[:, c, x, y], send_sem=csem.at[0], recv_sem=csem.at[1],
        device_id=(zs(m), e), device_id_type=MESH,
    )

    right, left = dev(zs(1), x, y, c), dev(zs(7), x, y, c)
    ring = [None, None]

    def zstep(w, s):
        if s > 1:
            for cp in ring[w]:
                cp.wait_recv()
        if s < 4:
            ra, la = zb.at[w, zs(9 - s)], zb.at[w, zs(s - 1)]
        elif s == 4:
            ra, la = zb.at[w, zs(5), 0], zb.at[w, zs(3), 1]
        else:
            return
        ring[w] = [send(ra, ra, right), send(la, la, left)]

    def step(a, d):
        own_rows[a].done((d,))
        for k in range(2):
            total = None
            for j in range(4):
                px, py = (j, ys(d)) if k == 0 else (xs(d), j)
                lhs = jnp.concatenate([xc[a, k, h, px, py] for h in range(2)], axis=1)
                cols = wide(px * NY + py)
                part = dot(lhs, win[k, cols, :]) if a == 0 else dot(lhs, wout[k, :, cols], 1, 1)
                total = part if total is None else total + part
            acc[a, k] = total if d == 0 else acc[a, k] + total

    for sp in own_rows:
        sp.first()

    @pl.when(away)
    def _():
        cross.start()

    @pl.when(jnp.logical_not(away))
    def _():
        xd[:, c, x, y] = cross_out[...]

    for sp in own_rows:
        sp.second()
    loads[2].wait()
    loads[3].wait()
    step(0, 0)
    own_rows[0].forward()
    step(1, 0)
    own_rows[1].forward()

    @pl.when(away)
    def _():
        cross.wait_recv()

    all_rows.first()
    step(0, 3)
    step(0, 1)
    own_rows[0].last()
    step(1, 3)
    step(0, 2)
    own_rows[1].last()
    for k in range(2):
        hidden = acc[0, k]
        tang = jnp.tanh(GELU_SCALE * (hidden + GELU_CUBIC * hidden * hidden * hidden))
        slope = 0.5 * (1.0 + tang) + 0.5 * hidden * (1.0 - tang * tang) * GELU_SCALE * (
            1.0 + 3.0 * GELU_CUBIC * hidden * hidden
        )
        acc[0, k] = slope
        zb[0, r, k] = (0.5 * hidden * (1.0 + tang)).astype(BF)
    zstep(0, 1)
    step(1, 1)
    step(1, 2)
    for k in range(2):
        zb[1, r, k] = (gate_col[k][:, 0:1] * acc[1, k] * acc[0, k]).astype(BF)
    zstep(1, 1)
    pair, stage1, stage2, gates_on_way, kept = {}, {0: [], 1: []}, {0: [], 1: []}, {}, {}
    outs = []

    def leave(src, dst):
        cp = pltpu.make_async_copy(src, dst, osem.at[len(outs)])
        cp.start()
        outs.append(cp)

    def slot_part(k):
        @pl.loop(0, NX)
        def _(i):
            for j in range(NY):
                part = dot(win[k, wide(i * NY + j), :], zb[1, r, k], 1, 1).astype(BF)
                for h in range(2):
                    ps[k, h, i, j] = part[h * COL : (h + 1) * COL]

        pair[k] = send(ps.at[k, oc], rsib.at[k], sib)

    def pair_sum(k):
        pair[k].wait_recv()

        @pl.loop(0, NX)
        def _(i):
            for j in range(NY):
                ps[k, c, i, j] = (ps[k, c, i, j].astype(F32) + rsib[k, i, j].astype(F32)).astype(BF)

        for d in (1, 3, 2):
            if k == 0:
                stage1[k].append(send(ps.at[0, c, xs(d)], rs1.at[0, x], dev(r, xs(d), y, c)))
            else:
                stage1[k].append(send(ps.at[1, c, :, ys(d)], rs1.at[1, y], dev(r, x, ys(d), c)))

    def first_sum(k):
        for cp in stage1[k]:
            cp.wait_recv()
        for j in range(4):
            total = (ps[0, c, x, j] if k == 0 else ps[1, c, j, y]).astype(F32)
            for d in (1, 2, 3):
                total += rs1[k, xs(d) if k == 0 else ys(d), j].astype(F32)
            ts[k, j] = total.astype(BF)
        for d in (1, 3, 2):
            if k == 0:
                stage2[k].append(send(ts.at[0, ys(d)], rs2.at[0, y], dev(r, x, ys(d), c)))
            else:
                stage2[k].append(send(ts.at[1, xs(d)], rs2.at[1, x], dev(r, xs(d), y, c)))

    def return_rows():
        expand = jnp.concatenate([hot(pos_row[k] == iota((PAD, CAP), 0)) for k in range(2)], axis=1)
        sums = []
        for k in range(2):
            for cp in stage2[k]:
                cp.wait_recv()
            total = ts[k, y if k == 0 else x].astype(F32)
            for d in (1, 2, 3):
                total += rs2[k, ys(d) if k == 0 else xs(d)].astype(F32)
            sums.append(total.astype(BF))
        sums = jnp.concatenate(sums, axis=1)
        ob[...] = dot(expand, sums, 1, 1).astype(BF).reshape(2, NX, NY, ROWS, COL)
        kept["back"] = plane(ob, rb, bsem, brsem)
        rb[c, x, y] = ob[c, x, y]

    def gate_sum(n):
        if n == 0:
            for k in range(2):
                gbuf[0, k] = lax.dot_general(
                    jnp.ones((8, F), F32), zb[0, r, k].astype(F32) * acc[1, k], (((1,), (1,)), ((), ())),
                    precision=lax.Precision.HIGHEST, preferred_element_type=F32,
                )
            gates_on_way[0] = [send(gbuf.at[0], gsib, sib)]
            return
        for cp in gates_on_way[n - 1]:
            cp.wait_recv()
        if n == 1:
            gbuf[1] = gbuf[0] + gsib[...]
            gx[x] = gbuf[1]
            gates_on_way[1] = [send(gbuf.at[1], gx.at[x], dev(r, xs(d), y, c)) for d in (1, 3, 2)]
        elif n == 2:
            gbuf[2] = (gx[0] + gx[1]) + (gx[2] + gx[3])
            gy[y] = gbuf[2]
            gates_on_way[2] = [send(gbuf.at[2], gy.at[y], dev(r, x, ys(d), c)) for d in (1, 3, 2)]
        else:
            total = (gy[0] + gy[1]) + (gy[2] + gy[3])
            for k in range(2):
                dgate_ref[0, k : k + 1, :] = total[k, 0:1, :]
            leave(dgate_ref, dgate_hbm)

    def column_spread(n):
        (None, None, all_rows.second, all_rows.forward, all_rows.last)[n]()

    def owner_pick():
        unpick = jnp.zeros((TOK, ROWS), F32)
        for k in range(2):
            bt = hot(ch_row[k] - e * TOK == iota((TOK, CAP), 0))
            at = hot(pos_col[k] - my_first == iota((CAP, ROWS), 1))
            unpick += dot(bt, at)
        unpick_ref[...] = unpick.astype(BF)
        leave(unpick_ref, unpick_hbm)

    steps = {
        "slot": slot_part, "pair": pair_sum, "sum": first_sum, "back": return_rows, "gate": gate_sum,
        "ring": zstep, "cols": column_spread, "pick": owner_pick,
    }
    for name, *at in ORDER:
        steps[name](*at)

    def factor(w, k):
        return jnp.concatenate([zb[w, zs((NZ - g) % NZ), k] for g in range(NZ)], axis=0)

    def columns(a, k, j):
        blocks = [
            jnp.concatenate([xd[k, h, g // 2, 2 * (g % 2) + j, a] for g in range(NZ)], axis=0)
            for h in range(2)
        ]
        return jnp.concatenate(blocks, axis=1)

    zstep(1, 5)
    all_rows.done()
    for k in range(2):
        for j in range(2):
            at = slice(j * 2 * COL, (j + 1) * 2 * COL)
            dwin_ref[k, at, :] = dot(columns(0, k, j), factor(1, k), 0, 0).astype(BF)
    leave(dwin_ref, dwin_hbm)
    zstep(0, 5)
    for k in range(2):
        for j in range(2):
            at = slice(j * 2 * COL, (j + 1) * 2 * COL)
            dwout_ref[k, :, at] = dot(factor(0, k), columns(1, k, j), 0, 0).astype(BF)
    leave(dwout_ref, dwout_hbm)

    for cp in kept["back"]:
        cp.wait_recv()

    @pl.loop(0, NX)
    def _(i):
        for j in range(NY):
            to = turned(i * NY + j)
            rows_out[:, to // NY, lax.rem(to, NY)] = rb[:, i, j]

    leave(rows_out, rows_hbm)

    assert counter[0] <= NSEM, counter[0]
    for cp in sent:
        cp.wait_send()

    for cp in forth + kept["back"]:
        cp.wait_send()
    for cp in outs:
        cp.wait()

    @pl.when(away)
    def _():
        cross.wait_send()


def finish(
    rows_hbm, unpick_hbm, gate_hbm, win_hbm, wout_hbm, dtok_hbm, dgate_hbm, dwin_hbm, dwout_hbm,
    rows, unpick, gate, win, wout, dtok, isem, osem,
):
    ins = [
        pltpu.make_async_copy(src, dst, isem.at[i])
        for i, (src, dst) in enumerate(
            ((rows_hbm, rows), (unpick_hbm, unpick), (gate_hbm, gate), (win_hbm, win), (wout_hbm, wout))
        )
    ]
    for cp in ins:
        cp.start()
    outs = []

    def leave(src, dst):
        cp = pltpu.make_async_copy(src, dst, osem.at[len(outs)])
        cp.start()
        outs.append(cp)

    ins[0].wait()
    ins[1].wait()
    for i in range(NX):
        block = jnp.concatenate([rows[h, i, j] for j in range(NY) for h in range(2)], axis=1)
        at = pl.ds(i * BLK, BLK)
        dtok[0, :, at] = dot(unpick[...], block).astype(BF)
        leave(dtok.at[0, :, at], dtok_hbm.at[0, :, at])
    for cp, src, dst in zip(ins[2:], (gate, win, wout), (dgate_hbm, dwin_hbm, dwout_hbm)):
        cp.wait()
        leave(src, dst)
    for cp in outs:
        cp.wait()


def local(tokens, grad_out, gates, chosen, w_in, w_out):
    hbm = pl.BlockSpec(memory_space=pl.ANY)
    vmem = pl.BlockSpec(memory_space=pltpu.VMEM)
    dma = pltpu.SemaphoreType.DMA
    d_gate = jax.ShapeDtypeStruct((1, 2, CAP), F32)
    d_in = jax.ShapeDtypeStruct((2, D // NZ, F), BF)
    d_out = jax.ShapeDtypeStruct((2, F, D // NZ), BF)
    parts = pl.pallas_call(
        kernel,
        out_shape=(
            jax.ShapeDtypeStruct((2, NX, NY, ROWS, COL), BF),
            jax.ShapeDtypeStruct((TOK, ROWS), BF),
            d_gate,
            d_in,
            d_out,
        ),
        in_specs=[hbm, hbm, vmem, vmem, hbm, hbm],
        out_specs=(hbm,) * 5,
        scratch_shapes=[
            pltpu.VMEM((TOK, ROWS), BF),
            pltpu.VMEM((1, 2, CAP), F32),
            pltpu.VMEM((2, D // NZ, F), BF),
            pltpu.VMEM((2, F, D // NZ), BF),
            pltpu.VMEM((TOK, D), BF),
            pltpu.VMEM((TOK, D), BF),
            pltpu.VMEM((2, D, F), BF),
            pltpu.VMEM((2, F, D), BF),
            pltpu.VMEM((2, NX, NY, 2, ROWS, COL), BF),
            pltpu.VMEM((2, NX, NY, 2, ROWS, COL), BF),
            pltpu.VMEM((2, 2, 2, NX, NY, CAP, COL), BF),
            pltpu.VMEM((2, 2, CAP, COL), BF),
            pltpu.VMEM((2, 2, NX, NY, 2, CAP, COL), BF),
            pltpu.VMEM((2, NZ, 2, CAP, F), BF),
            pltpu.VMEM((2, 2, CAP, F), F32),
            pltpu.VMEM((2, 2, NX, NY, CAP, COL), BF),
            pltpu.VMEM((2, NX, NY, CAP, COL), BF),
            pltpu.VMEM((2, 4, 4, CAP, COL), BF),
            pltpu.VMEM((2, 4, CAP, COL), BF),
            pltpu.VMEM((2, 4, CAP, COL), BF),
            pltpu.VMEM((2, NX, NY, ROWS, COL), BF),
            pltpu.VMEM((2, NX, NY, ROWS, COL), BF),
            pltpu.VMEM((2, NX, NY, ROWS, COL), BF),
            pltpu.VMEM((3, 2, 8, CAP), F32),
            pltpu.VMEM((2, 8, CAP), F32),
            pltpu.VMEM((4, 2, 8, CAP), F32),
            pltpu.VMEM((4, 2, 8, CAP), F32),
            dma((NSEM,)),
            dma((NSEM,)),
            dma((PLANE,)),
            dma((PLANE,)),
            dma((PLANE,)),
            dma((PLANE,)),
            dma((4,)),
            dma((5,)),
            dma((2,)),
        ],
        compiler_params=pltpu.CompilerParams(
            collective_id=0, has_side_effects=True, vmem_limit_bytes=60 << 20
        ),
        name="expert_backward",
    )(tokens, grad_out, gates, chosen, w_in, w_out)
    return pl.pallas_call(
        finish,
        out_shape=(jax.ShapeDtypeStruct((1, TOK, D), BF), d_gate, d_in, d_out),
        in_specs=[hbm] * 5,
        out_specs=(hbm,) * 4,
        scratch_shapes=[
            pltpu.VMEM((2, NX, NY, ROWS, COL), BF),
            pltpu.VMEM((TOK, ROWS), BF),
            pltpu.VMEM((1, 2, CAP), F32),
            pltpu.VMEM((2, D // NZ, F), BF),
            pltpu.VMEM((2, F, D // NZ), BF),
            pltpu.VMEM((1, TOK, D), BF),
            dma((5,)),
            dma((7,)),
        ],
        compiler_params=pltpu.CompilerParams(vmem_limit_bytes=60 << 20),
        name="finish",
    )(*parts)


def solution(mesh):
    return jax.shard_map(
        local,
        mesh=mesh,
        in_specs=(
            P("rep", "exp", None),
            P("rep", "exp", None),
            P("rep", None, None),
            P("rep", None, None),
            P(None, None, "exp"),
            P(None, "exp", None),
        ),
        out_specs=(
            P("rep", "exp", None),
            P("rep", None, None),
            P(None, "rep", "exp"),
            P(None, "exp", "rep"),
        ),
        check_vma=False,
    )
```

```python
import jax
import jax.numpy as jnp
from jax import lax
from jax.experimental import pallas as pl
from jax.experimental.pallas import tpu as pltpu
from jax.sharding import PartitionSpec as P

GELU_SCALE = 0.7978845608028654
GELU_CUBIC = 0.044715

BF = jnp.bfloat16
F32 = jnp.float32
MESH = pl.DeviceIdType.MESH

NX, NY, NZ = 4, 4, 8
D = 4096
F = 256
CAP = 128
TOK = 128
MOST = 8
ROWS = 2 * MOST
PAD = NX * NY * 2 * ROWS
COL = 128
BLK = D // NX
PLANE = NX * NY * 2

NSEM = 144

ORDER = (
    ("cols", 2), ("slot", 0), ("ring", 0, 2), ("slot", 1), ("gate", 0), ("pair", 0), ("pair", 1), ("ring", 1, 2), ("cols", 3), ("gate", 1), ("ring", 0, 3), ("ring", 1, 3), ("sum", 0), ("sum", 1), ("ring", 0, 4), ("gate", 2), ("ring", 1, 4), ("cols", 4), ("back",), ("pick",), ("gate", 3),
)


def dot(a, b, ca=1, cb=0):
    return lax.dot_general(a, b, (((ca,), (cb,)), ((), ())), preferred_element_type=F32)


def kernel(
    tok_hbm, grad_hbm, gates_ref, chosen_ref, win_hbm, wout_hbm,
    rows_hbm, unpick_hbm, dgate_hbm, dwin_hbm, dwout_hbm,
    unpick_ref, dgate_ref, dwin_ref, dwout_ref, tok, grad, win, wout, pk, rp, xc, cross_out, xd, zb, acc, ps, rsib, rs1, ts, rs2, ob, rb, rows_out,
    gbuf, gsib, gx, gy,
    ssem, rsem, asem, arsem, bsem, brsem, lsem, osem, csem,
):
    r = lax.axis_index("rep")
    e = lax.axis_index("exp")
    x = e // 8
    y = (e // 2) % 4
    c = e % 2
    oc = 1 - c
    chip = x * NY + y

    def dev(rr, xx, yy, c_):
        return (rr, (xx * 4 + yy) * 2 + c_)

    def xs(d):
        return lax.rem(x + d, 4)

    def ys(d):
        return lax.rem(y + d, 4)

    def zs(d):
        return lax.rem(r + d, 8)

    sib = dev(r, x, y, oc)

    loads = [
        pltpu.make_async_copy(tok_hbm.at[0], tok, lsem.at[0]),
        pltpu.make_async_copy(grad_hbm.at[0], grad, lsem.at[1]),
        pltpu.make_async_copy(win_hbm, win, lsem.at[2]),
        pltpu.make_async_copy(wout_hbm, wout, lsem.at[3]),
    ]
    loads[0].start()
    loads[1].start()

    barrier = pltpu.get_barrier_semaphore()

    for i in range(1, PLANE):
        to = dev(r, xs(i // 8), ys((i // 2) % 4), oc if i % 2 else c)
        pl.semaphore_signal(barrier, inc=1, device_id=to, device_id_type=MESH)
    for d in range(1, NZ):
        pl.semaphore_signal(barrier, inc=1, device_id=dev(zs(d), x, y, c), device_id_type=MESH)

    m = e // 4
    away = m != 0

    def turned(p):
        return lax.rem(p + 2 * r, NX * NY)
    counter = [0]
    sent = []

    def send(src, dst, to):
        i = counter[0]
        counter[0] += 1
        cp = pltpu.make_async_remote_copy(
            src_ref=src, dst_ref=dst, send_sem=ssem.at[i], recv_sem=rsem.at[i],
            device_id=to, device_id_type=MESH,
        )
        cp.start()
        sent.append(cp)
        return cp

    def iota(shape, dim):
        return lax.broadcasted_iota(jnp.int32, shape, dim)

    def hot(m):
        return jnp.where(m, 1.0, 0.0).astype(BF)

    sq = (CAP, CAP)
    my_first = (c * (NX * NY) + chip) * ROWS
    ch_row, ch_col, pos_row, pos_col, gate_col = [], [], [], [], []
    for k in range(2):
        row = chosen_ref[0, k : k + 1, :]
        rb_ = jnp.broadcast_to(row, sq)
        cb_ = rb_.T
        same = (rb_ // TOK) == (cb_ // TOK)
        rank_col = jnp.sum(jnp.where(same & (iota(sq, 1) < iota(sq, 0)), 1, 0), axis=1, keepdims=True)
        rank_row = jnp.sum(jnp.where(same & (iota(sq, 0) < iota(sq, 1)), 1, 0), axis=0, keepdims=True)

        def place(own, rank):
            return ((own % 2) * (NX * NY) + own // 2) * ROWS + k * MOST + rank

        ch_row.append(row)
        ch_col.append(cb_[:, 0:1])
        pos_row.append(place(row // TOK, rank_row))
        pos_col.append(place(cb_[:, 0:1] // TOK, rank_col))

    pick = jnp.zeros((ROWS, TOK), F32)
    for k in range(2):
        a = hot(pos_row[k] - my_first == iota((ROWS, CAP), 0))
        b = hot(ch_col[k] - e * TOK == iota((CAP, TOK), 1))
        pick += dot(a, b)
    pick = pick.astype(BF)

    loads[0].wait()
    loads[1].wait()
    loads[2].start()
    loads[3].start()

    def wide(p):
        return pl.ds(pl.multiple_of(turned(p) * 2 * COL, 2 * COL), 2 * COL)

    @pl.loop(0, NX)
    def _(i):
        for j in range(NY):
            cols = wide(i * NY + j)
            xr = dot(pick, tok[:, cols]).astype(BF)
            dr = dot(pick, grad[:, cols]).astype(BF)
            for k in range(2):
                pk[k, i, j, 0] = xr[:, k * COL : (k + 1) * COL]
                pk[k, i, j, 1] = dr[:, k * COL : (k + 1) * COL]

    pl.semaphore_wait(barrier, PLANE - 1 + NZ - 1)


    def plane(src, dst, s_sem, r_sem):
        copies = []
        for i in range(1, PLANE):
            px, py, pc = xs(i // 8), ys((i // 2) % 4), (oc if i % 2 else c)
            cp = pltpu.make_async_remote_copy(
                src_ref=src.at[pc, px, py], dst_ref=dst.at[c, x, y], send_sem=s_sem.at[i],
                recv_sem=r_sem.at[i], device_id=dev(r, px, py, pc), device_id_type=MESH,
            )
            cp.start()
            copies.append(cp)
        return copies

    forth = plane(pk, rp, asem, arsem)
    rp[c, x, y] = pk[c, x, y]
    gather = jnp.concatenate([hot(pos_col[k] == iota((CAP, PAD), 1)) for k in range(2)], axis=0)
    for k in range(2):
        gate_col.append(jnp.broadcast_to(gates_ref[0, k : k + 1, :], sq).T)

    for cp in forth:
        cp.wait_recv()

    both = jnp.concatenate([rp[:, :, :, k].reshape(PAD, COL) for k in range(2)], axis=1)
    both = dot(gather, both)
    for a in range(2):
        for k in range(2):
            block = both[k * CAP : (k + 1) * CAP, a * COL : (a + 1) * COL]
            xc[a, k, c, x, y] = block.astype(BF)
            cross_out[k, a] = (block if a == 0 else gate_col[k] * block).astype(BF)

    class Spread:
        def __init__(self, row):
            self.row = row

        def block(self, k):
            return self.row(k, 0, x if k == 0 else y)

        def first(self):
            self.got = []
            for d in (1, 3, 2):
                for k, to in ((0, dev(r, xs(d), y, c)), (1, dev(r, x, ys(d), c))):
                    ref = self.block(k)
                    self.got.append(send(ref, ref, to))

        def along(self, k, d):
            return dev(r, x, ys(d), c) if k == 0 else dev(r, xs(d), y, c)

        def second(self):
            for cp in self.got:
                cp.wait_recv()
            self.got = []
            for k in range(2):
                ref = self.row(k, 0, slice(0, 4))
                for d in (1, 3):
                    self.got.append(send(ref, ref, self.along(k, d)))
            self.sibs = {}
            self.share(0)

        def forward(self):
            got, self.got = self.got, []
            for k in range(2):
                for n, (d, at) in enumerate(((3, slice(0, 2)), (1, slice(2, 4)))):
                    got[2 * k + n].wait_recv()
                    ref = self.row(k, d, at)
                    self.got.append(send(ref, ref, self.along(k, 1 if d == 3 else 3)))
            self.share(3)
            self.share(1)

        def share(self, d):
            refs = [self.row(k, d, slice(0, 4)) for k in range(2)]
            self.sibs[d] = [send(ref, ref, sib) for ref in refs]

        def last(self):
            for cp in self.got:
                cp.wait_recv()
            self.share(2)

        def done(self, rows=(0, 3, 1, 2)):
            for d in rows:
                for cp in self.sibs[d]:
                    cp.wait_recv()

    def rows_of(a):
        return lambda k, d, at: xc.at[a, 0, c, at, ys(d)] if k == 0 else xc.at[a, 1, c, xs(d), at]

    def columns(k, d, at):
        return xd.at[0, c, at, ys(d)] if k == 0 else xd.at[1, c, xs(d), at]

    own_rows = [Spread(rows_of(a)) for a in range(2)]
    all_rows = Spread(columns)

    cross = pltpu.make_async_remote_copy(
        src_ref=cross_out, dst_ref=xd.at[:, c, x, y], send_sem=csem.at[0], recv_sem=csem.at[1],
        device_id=(zs(m), e), device_id_type=MESH,
    )

    right, left = dev(zs(1), x, y, c), dev(zs(7), x, y, c)
    ring = [None, None]

    def zstep(w, s):
        if s > 1:
            for cp in ring[w]:
                cp.wait_recv()
        if s < 4:
            ra, la = zb.at[w, zs(9 - s)], zb.at[w, zs(s - 1)]
        elif s == 4:
            ra, la = zb.at[w, zs(5), 0], zb.at[w, zs(3), 1]
        else:
            return
        ring[w] = [send(ra, ra, right), send(la, la, left)]

    def step(a, d):
        own_rows[a].done((d,))
        for k in range(2):
            total = None
            for j in range(4):
                px, py = (j, ys(d)) if k == 0 else (xs(d), j)
                lhs = jnp.concatenate([xc[a, k, h, px, py] for h in range(2)], axis=1)
                cols = wide(px * NY + py)
                part = dot(lhs, win[k, cols, :]) if a == 0 else dot(lhs, wout[k, :, cols], 1, 1)
                total = part if total is None else total + part
            acc[a, k] = total if d == 0 else acc[a, k] + total

    for sp in own_rows:
        sp.first()

    @pl.when(away)
    def _():
        cross.start()

    @pl.when(jnp.logical_not(away))
    def _():
        xd[:, c, x, y] = cross_out[...]

    for sp in own_rows:
        sp.second()
    loads[2].wait()
    loads[3].wait()
    step(0, 0)
    own_rows[0].forward()
    step(1, 0)
    own_rows[1].forward()

    step(0, 3)
    step(0, 1)
    own_rows[0].last()
    @pl.when(away)
    def _():
        cross.wait_recv()

    all_rows.first()
    step(1, 3)
    step(0, 2)
    own_rows[1].last()
    for k in range(2):
        hidden = acc[0, k]
        tang = jnp.tanh(GELU_SCALE * (hidden + GELU_CUBIC * hidden * hidden * hidden))
        slope = 0.5 * (1.0 + tang) + 0.5 * hidden * (1.0 - tang * tang) * GELU_SCALE * (
            1.0 + 3.0 * GELU_CUBIC * hidden * hidden
        )
        acc[0, k] = slope
        zb[0, r, k] = (0.5 * hidden * (1.0 + tang)).astype(BF)
    zstep(0, 1)
    step(1, 1)
    step(1, 2)
    for k in range(2):
        zb[1, r, k] = (gate_col[k][:, 0:1] * acc[1, k] * acc[0, k]).astype(BF)
    zstep(1, 1)
    pair, stage1, stage2, gates_on_way, kept = {}, {0: [], 1: []}, {0: [], 1: []}, {}, {}
    outs = []

    def leave(src, dst):
        cp = pltpu.make_async_copy(src, dst, osem.at[len(outs)])
        cp.start()
        outs.append(cp)

    def slot_part(k):
        pair[k] = []
        for n in range(2):

            @pl.loop(2 * n, 2 * n + 2)
            def _(i):
                for j in range(NY):
                    part = dot(win[k, wide(i * NY + j), :], zb[1, r, k], 1, 1).astype(BF)
                    for h in range(2):
                        ps[k, h, i, j] = part[h * COL : (h + 1) * COL]

            at = slice(2 * n, 2 * n + 2)
            pair[k].append(send(ps.at[k, oc, at], rsib.at[k, at], sib))

    def pair_sum(k):
        for n in range(2):
            pair[k][n].wait_recv()

            @pl.loop(2 * n, 2 * n + 2)
            def _(i):
                for j in range(NY):
                    ps[k, c, i, j] = (ps[k, c, i, j].astype(F32) + rsib[k, i, j].astype(F32)).astype(BF)

        for d in (1, 3, 2):
            if k == 0:
                stage1[k].append(send(ps.at[0, c, xs(d)], rs1.at[0, x], dev(r, xs(d), y, c)))
            else:
                stage1[k].append(send(ps.at[1, c, :, ys(d)], rs1.at[1, y], dev(r, x, ys(d), c)))

    def first_sum(k):
        for cp in stage1[k]:
            cp.wait_recv()
        for j in range(4):
            total = (ps[0, c, x, j] if k == 0 else ps[1, c, j, y]).astype(F32)
            for d in (1, 2, 3):
                total += rs1[k, xs(d) if k == 0 else ys(d), j].astype(F32)
            ts[k, j] = total.astype(BF)
        for d in (1, 3, 2):
            if k == 0:
                stage2[k].append(send(ts.at[0, ys(d)], rs2.at[0, y], dev(r, x, ys(d), c)))
            else:
                stage2[k].append(send(ts.at[1, xs(d)], rs2.at[1, x], dev(r, xs(d), y, c)))

    def return_rows():
        expand = jnp.concatenate([hot(pos_row[k] == iota((PAD, CAP), 0)) for k in range(2)], axis=1)
        sums = []
        for k in range(2):
            for cp in stage2[k]:
                cp.wait_recv()
            total = ts[k, y if k == 0 else x].astype(F32)
            for d in (1, 2, 3):
                total += rs2[k, ys(d) if k == 0 else xs(d)].astype(F32)
            sums.append(total.astype(BF))
        sums = jnp.concatenate(sums, axis=1)
        ob[...] = dot(expand, sums, 1, 1).astype(BF).reshape(2, NX, NY, ROWS, COL)
        kept["back"] = plane(ob, rb, bsem, brsem)
        rb[c, x, y] = ob[c, x, y]

    def gate_sum(n):
        if n == 0:
            for k in range(2):
                gbuf[0, k] = lax.dot_general(
                    jnp.ones((8, F), F32), zb[0, r, k].astype(F32) * acc[1, k], (((1,), (1,)), ((), ())),
                    precision=lax.Precision.HIGHEST, preferred_element_type=F32,
                )
            gates_on_way[0] = [send(gbuf.at[0], gsib, sib)]
            return
        for cp in gates_on_way[n - 1]:
            cp.wait_recv()
        if n == 1:
            gbuf[1] = gbuf[0] + gsib[...]
            gx[x] = gbuf[1]
            gates_on_way[1] = [send(gbuf.at[1], gx.at[x], dev(r, xs(d), y, c)) for d in (1, 3, 2)]
        elif n == 2:
            gbuf[2] = (gx[0] + gx[1]) + (gx[2] + gx[3])
            gy[y] = gbuf[2]
            gates_on_way[2] = [send(gbuf.at[2], gy.at[y], dev(r, x, ys(d), c)) for d in (1, 3, 2)]
        else:
            total = (gy[0] + gy[1]) + (gy[2] + gy[3])
            for k in range(2):
                dgate_ref[0, k : k + 1, :] = total[k, 0:1, :]
            leave(dgate_ref, dgate_hbm)

    def column_spread(n):
        (None, None, all_rows.second, all_rows.forward, all_rows.last)[n]()

    def owner_pick():
        unpick = jnp.zeros((TOK, ROWS), F32)
        for k in range(2):
            bt = hot(ch_row[k] - e * TOK == iota((TOK, CAP), 0))
            at = hot(pos_col[k] - my_first == iota((CAP, ROWS), 1))
            unpick += dot(bt, at)
        unpick_ref[...] = unpick.astype(BF)
        leave(unpick_ref, unpick_hbm)

    steps = {
        "slot": slot_part, "pair": pair_sum, "sum": first_sum, "back": return_rows, "gate": gate_sum,
        "ring": zstep, "cols": column_spread, "pick": owner_pick,
    }
    for name, *at in ORDER:
        steps[name](*at)

    def factor(w, k):
        return jnp.concatenate([zb[w, zs((NZ - g) % NZ), k] for g in range(NZ)], axis=0)

    def columns(a, k, j):
        blocks = [
            jnp.concatenate([xd[k, h, g // 2, 2 * (g % 2) + j, a] for g in range(NZ)], axis=0)
            for h in range(2)
        ]
        return jnp.concatenate(blocks, axis=1)

    zstep(0, 5)
    all_rows.done()
    for k in range(2):
        for j in range(2):
            at = slice(j * 2 * COL, (j + 1) * 2 * COL)
            dwout_ref[k, :, at] = dot(factor(0, k), columns(1, k, j), 0, 0).astype(BF)
    leave(dwout_ref, dwout_hbm)
    zstep(1, 5)
    for k in range(2):
        for j in range(2):
            at = slice(j * 2 * COL, (j + 1) * 2 * COL)
            dwin_ref[k, at, :] = dot(columns(0, k, j), factor(1, k), 0, 0).astype(BF)
    leave(dwin_ref, dwin_hbm)

    assert counter[0] <= NSEM, counter[0]
    for cp in sent + forth:
        cp.wait_send()

    @pl.when(away)
    def _():
        cross.wait_send()

    for cp in kept["back"]:
        cp.wait_recv()

    @pl.loop(0, NX)
    def _(i):
        for j in range(NY):
            to = turned(i * NY + j)
            rows_out[:, to // NY, lax.rem(to, NY)] = rb[:, i, j]

    leave(rows_out, rows_hbm)

    for cp in kept["back"]:
        cp.wait_send()
    for cp in outs:
        cp.wait()


def finish(
    rows_hbm, unpick_hbm, gate_hbm, win_hbm, wout_hbm, dtok_hbm, dgate_hbm, dwin_hbm, dwout_hbm,
    rows, unpick, gate, win, wout, dtok, isem, osem,
):
    ins = [
        pltpu.make_async_copy(src, dst, isem.at[i])
        for i, (src, dst) in enumerate(
            ((rows_hbm, rows), (unpick_hbm, unpick), (gate_hbm, gate), (win_hbm, win), (wout_hbm, wout))
        )
    ]
    for cp in ins:
        cp.start()
    outs = []

    def leave(src, dst):
        cp = pltpu.make_async_copy(src, dst, osem.at[len(outs)])
        cp.start()
        outs.append(cp)

    ins[0].wait()
    ins[1].wait()
    for i in range(NX):
        block = jnp.concatenate([rows[h, i, j] for j in range(NY) for h in range(2)], axis=1)
        at = pl.ds(i * BLK, BLK)
        dtok[0, :, at] = dot(unpick[...], block).astype(BF)
        leave(dtok.at[0, :, at], dtok_hbm.at[0, :, at])
    for cp, src, dst in zip(ins[2:], (gate, win, wout), (dgate_hbm, dwin_hbm, dwout_hbm)):
        cp.wait()
        leave(src, dst)
    for cp in outs:
        cp.wait()


def local(tokens, grad_out, gates, chosen, w_in, w_out):
    hbm = pl.BlockSpec(memory_space=pl.ANY)
    vmem = pl.BlockSpec(memory_space=pltpu.VMEM)
    dma = pltpu.SemaphoreType.DMA
    d_gate = jax.ShapeDtypeStruct((1, 2, CAP), F32)
    d_in = jax.ShapeDtypeStruct((2, D // NZ, F), BF)
    d_out = jax.ShapeDtypeStruct((2, F, D // NZ), BF)
    parts = pl.pallas_call(
        kernel,
        out_shape=(
            jax.ShapeDtypeStruct((2, NX, NY, ROWS, COL), BF),
            jax.ShapeDtypeStruct((TOK, ROWS), BF),
            d_gate,
            d_in,
            d_out,
        ),
        in_specs=[hbm, hbm, vmem, vmem, hbm, hbm],
        out_specs=(hbm,) * 5,
        scratch_shapes=[
            pltpu.VMEM((TOK, ROWS), BF),
            pltpu.VMEM((1, 2, CAP), F32),
            pltpu.VMEM((2, D // NZ, F), BF),
            pltpu.VMEM((2, F, D // NZ), BF),
            pltpu.VMEM((TOK, D), BF),
            pltpu.VMEM((TOK, D), BF),
            pltpu.VMEM((2, D, F), BF),
            pltpu.VMEM((2, F, D), BF),
            pltpu.VMEM((2, NX, NY, 2, ROWS, COL), BF),
            pltpu.VMEM((2, NX, NY, 2, ROWS, COL), BF),
            pltpu.VMEM((2, 2, 2, NX, NY, CAP, COL), BF),
            pltpu.VMEM((2, 2, CAP, COL), BF),
            pltpu.VMEM((2, 2, NX, NY, 2, CAP, COL), BF),
            pltpu.VMEM((2, NZ, 2, CAP, F), BF),
            pltpu.VMEM((2, 2, CAP, F), F32),
            pltpu.VMEM((2, 2, NX, NY, CAP, COL), BF),
            pltpu.VMEM((2, NX, NY, CAP, COL), BF),
            pltpu.VMEM((2, 4, 4, CAP, COL), BF),
            pltpu.VMEM((2, 4, CAP, COL), BF),
            pltpu.VMEM((2, 4, CAP, COL), BF),
            pltpu.VMEM((2, NX, NY, ROWS, COL), BF),
            pltpu.VMEM((2, NX, NY, ROWS, COL), BF),
            pltpu.VMEM((2, NX, NY, ROWS, COL), BF),
            pltpu.VMEM((3, 2, 8, CAP), F32),
            pltpu.VMEM((2, 8, CAP), F32),
            pltpu.VMEM((4, 2, 8, CAP), F32),
            pltpu.VMEM((4, 2, 8, CAP), F32),
            dma((NSEM,)),
            dma((NSEM,)),
            dma((PLANE,)),
            dma((PLANE,)),
            dma((PLANE,)),
            dma((PLANE,)),
            dma((4,)),
            dma((5,)),
            dma((2,)),
        ],
        compiler_params=pltpu.CompilerParams(
            collective_id=0, has_side_effects=True, vmem_limit_bytes=60 << 20
        ),
        name="expert_backward",
    )(tokens, grad_out, gates, chosen, w_in, w_out)
    return pl.pallas_call(
        finish,
        out_shape=(jax.ShapeDtypeStruct((1, TOK, D), BF), d_gate, d_in, d_out),
        in_specs=[hbm] * 5,
        out_specs=(hbm,) * 4,
        scratch_shapes=[
            pltpu.VMEM((2, NX, NY, ROWS, COL), BF),
            pltpu.VMEM((TOK, ROWS), BF),
            pltpu.VMEM((1, 2, CAP), F32),
            pltpu.VMEM((2, D // NZ, F), BF),
            pltpu.VMEM((2, F, D // NZ), BF),
            pltpu.VMEM((1, TOK, D), BF),
            dma((5,)),
            dma((7,)),
        ],
        compiler_params=pltpu.CompilerParams(vmem_limit_bytes=60 << 20),
        name="finish",
    )(*parts)


def solution(mesh):
    return jax.shard_map(
        local,
        mesh=mesh,
        in_specs=(
            P("rep", "exp", None),
            P("rep", "exp", None),
            P("rep", None, None),
            P("rep", None, None),
            P(None, None, "exp"),
            P(None, "exp", None),
        ),
        out_specs=(
            P("rep", "exp", None),
            P("rep", None, None),
            P(None, "rep", "exp"),
            P(None, "exp", "rep"),
        ),
        check_vma=False,
    )
```

```python
import jax
import jax.numpy as jnp
from jax import lax
from jax.experimental import pallas as pl
from jax.experimental.pallas import tpu as pltpu
from jax.sharding import PartitionSpec as P

GELU_SCALE = 0.7978845608028654
GELU_CUBIC = 0.044715

BF = jnp.bfloat16
F32 = jnp.float32
MESH = pl.DeviceIdType.MESH

NX, NY, NZ = 4, 4, 8
D = 4096
F = 256
CAP = 128
TOK = 128
MOST = 8
ROWS = 2 * MOST
PAD = NX * NY * 2 * ROWS
COL = 128
BLK = D // NX
PLANE = NX * NY * 2

NSEM = 144

ORDER = (
    ("cols", 2), ("slot", 0), ("ring", 0, 2), ("slot", 1), ("gate", 0), ("pair", 0), ("pair", 1), ("ring", 1, 2), ("cols", 3), ("gate", 1), ("ring", 0, 3), ("ring", 1, 3), ("sum", 0), ("sum", 1), ("ring", 0, 4), ("gate", 2), ("ring", 1, 4), ("cols", 4), ("back",), ("pick",), ("gate", 3),
)


def dot(a, b, ca=1, cb=0):
    return lax.dot_general(a, b, (((ca,), (cb,)), ((), ())), preferred_element_type=F32)


def kernel(
    tok_hbm, grad_hbm, gates_ref, chosen_ref, win_hbm, wout_hbm,
    rows_hbm, unpick_hbm, dgate_hbm, dwin_hbm, dwout_hbm,
    unpick_ref, dgate_ref, dwin_ref, dwout_ref, tok, grad, win, wout, pk, rp, xc, cross_out, xd, zb, acc, ps, rsib, rs1, ts, rs2, ob, rb, rows_out,
    gbuf, gsib, gx, gy,
    ssem, rsem, asem, arsem, bsem, brsem, lsem, osem, csem,
):
    r = lax.axis_index("rep")
    e = lax.axis_index("exp")
    x = e // 8
    y = (e // 2) % 4
    c = e % 2
    oc = 1 - c
    chip = x * NY + y

    def dev(rr, xx, yy, c_):
        return (rr, (xx * 4 + yy) * 2 + c_)

    def xs(d):
        return lax.rem(x + d, 4)

    def ys(d):
        return lax.rem(y + d, 4)

    def zs(d):
        return lax.rem(r + d, 8)

    sib = dev(r, x, y, oc)

    loads = [
        pltpu.make_async_copy(tok_hbm.at[0], tok, lsem.at[0]),
        pltpu.make_async_copy(grad_hbm.at[0], grad, lsem.at[1]),
        pltpu.make_async_copy(win_hbm, win, lsem.at[2]),
        pltpu.make_async_copy(wout_hbm, wout, lsem.at[3]),
    ]
    loads[0].start()
    loads[1].start()

    barrier = pltpu.get_barrier_semaphore()

    for i in range(1, PLANE):
        to = dev(r, xs(i // 8), ys((i // 2) % 4), oc if i % 2 else c)
        pl.semaphore_signal(barrier, inc=1, device_id=to, device_id_type=MESH)
    for d in range(1, NZ):
        pl.semaphore_signal(barrier, inc=1, device_id=dev(zs(d), x, y, c), device_id_type=MESH)

    m = e // 4
    away = m != 0

    def turned(p):
        return lax.rem(p + 2 * r, NX * NY)
    counter = [0]
    sent = []

    def send(src, dst, to):
        i = counter[0]
        counter[0] += 1
        cp = pltpu.make_async_remote_copy(
            src_ref=src, dst_ref=dst, send_sem=ssem.at[i], recv_sem=rsem.at[i],
            device_id=to, device_id_type=MESH,
        )
        cp.start()
        sent.append(cp)
        return cp

    def iota(shape, dim):
        return lax.broadcasted_iota(jnp.int32, shape, dim)

    def hot(m):
        return jnp.where(m, 1.0, 0.0).astype(BF)

    sq = (CAP, CAP)
    my_first = (c * (NX * NY) + chip) * ROWS
    ch_row, ch_col, pos_row, pos_col, gate_col = [], [], [], [], []
    for k in range(2):
        row = chosen_ref[0, k : k + 1, :]
        rb_ = jnp.broadcast_to(row, sq)
        cb_ = rb_.T
        same = (rb_ // TOK) == (cb_ // TOK)
        rank_col = jnp.sum(jnp.where(same & (iota(sq, 1) < iota(sq, 0)), 1, 0), axis=1, keepdims=True)
        rank_row = jnp.sum(jnp.where(same & (iota(sq, 0) < iota(sq, 1)), 1, 0), axis=0, keepdims=True)

        def place(own, rank):
            return ((own % 2) * (NX * NY) + own // 2) * ROWS + k * MOST + rank

        ch_row.append(row)
        ch_col.append(cb_[:, 0:1])
        pos_row.append(place(row // TOK, rank_row))
        pos_col.append(place(cb_[:, 0:1] // TOK, rank_col))

    pick = jnp.zeros((ROWS, TOK), F32)
    for k in range(2):
        a = hot(pos_row[k] - my_first == iota((ROWS, CAP), 0))
        b = hot(ch_col[k] - e * TOK == iota((CAP, TOK), 1))
        pick += dot(a, b)
    pick = pick.astype(BF)

    def wide(p):
        return pl.ds(pl.multiple_of(turned(p) * 2 * COL, 2 * COL), 2 * COL)

    for a, source in enumerate((tok, grad)):
        loads[a].wait()

        @pl.loop(0, NX)
        def _(i):
            for j in range(NY):
                packed = dot(pick, source[:, wide(i * NY + j)]).astype(BF)
                for k in range(2):
                    pk[k, i, j, a] = packed[:, k * COL : (k + 1) * COL]

    loads[2].start()
    loads[3].start()
    pl.semaphore_wait(barrier, PLANE - 1 + NZ - 1)


    def plane(src, dst, s_sem, r_sem):
        copies = []
        for i in range(1, PLANE):
            px, py, pc = xs(i // 8), ys((i // 2) % 4), (oc if i % 2 else c)
            cp = pltpu.make_async_remote_copy(
                src_ref=src.at[pc, px, py], dst_ref=dst.at[c, x, y], send_sem=s_sem.at[i],
                recv_sem=r_sem.at[i], device_id=dev(r, px, py, pc), device_id_type=MESH,
            )
            cp.start()
            copies.append(cp)
        return copies

    forth = plane(pk, rp, asem, arsem)
    rp[c, x, y] = pk[c, x, y]
    gather = jnp.concatenate([hot(pos_col[k] == iota((CAP, PAD), 1)) for k in range(2)], axis=0)
    for k in range(2):
        gate_col.append(jnp.broadcast_to(gates_ref[0, k : k + 1, :], sq).T)

    for cp in forth:
        cp.wait_recv()

    both = jnp.concatenate([rp[:, :, :, k].reshape(PAD, COL) for k in range(2)], axis=1)
    both = dot(gather, both)
    for a in range(2):
        for k in range(2):
            block = both[k * CAP : (k + 1) * CAP, a * COL : (a + 1) * COL]
            xc[a, k, c, x, y] = block.astype(BF)
            cross_out[k, a] = (block if a == 0 else gate_col[k] * block).astype(BF)

    class Spread:
        def __init__(self, row):
            self.row = row

        def block(self, k):
            return self.row(k, 0, x if k == 0 else y)

        def first(self):
            self.got = []
            for d in (1, 3, 2):
                for k, to in ((0, dev(r, xs(d), y, c)), (1, dev(r, x, ys(d), c))):
                    ref = self.block(k)
                    self.got.append(send(ref, ref, to))

        def along(self, k, d):
            return dev(r, x, ys(d), c) if k == 0 else dev(r, xs(d), y, c)

        def second(self):
            for cp in self.got:
                cp.wait_recv()
            self.got = []
            for k in range(2):
                ref = self.row(k, 0, slice(0, 4))
                for d in (1, 3):
                    self.got.append(send(ref, ref, self.along(k, d)))
            self.sibs = {}
            self.share(0)

        def forward(self):
            got, self.got = self.got, []
            for k in range(2):
                for n, (d, at) in enumerate(((3, slice(0, 2)), (1, slice(2, 4)))):
                    got[2 * k + n].wait_recv()
                    ref = self.row(k, d, at)
                    self.got.append(send(ref, ref, self.along(k, 1 if d == 3 else 3)))
            self.share(3)
            self.share(1)

        def share(self, d):
            refs = [self.row(k, d, slice(0, 4)) for k in range(2)]
            self.sibs[d] = [send(ref, ref, sib) for ref in refs]

        def last(self):
            for cp in self.got:
                cp.wait_recv()
            self.share(2)

        def done(self, rows=(0, 3, 1, 2)):
            for d in rows:
                for cp in self.sibs[d]:
                    cp.wait_recv()

    def rows_of(a):
        return lambda k, d, at: xc.at[a, 0, c, at, ys(d)] if k == 0 else xc.at[a, 1, c, xs(d), at]

    def columns(k, d, at):
        return xd.at[0, c, at, ys(d)] if k == 0 else xd.at[1, c, xs(d), at]

    own_rows = [Spread(rows_of(a)) for a in range(2)]
    all_rows = Spread(columns)

    cross = pltpu.make_async_remote_copy(
        src_ref=cross_out, dst_ref=xd.at[:, c, x, y], send_sem=csem.at[0], recv_sem=csem.at[1],
        device_id=(zs(m), e), device_id_type=MESH,
    )

    right, left = dev(zs(1), x, y, c), dev(zs(7), x, y, c)
    ring = [None, None]

    def zstep(w, s):
        if s > 1:
            for cp in ring[w]:
                cp.wait_recv()
        if s < 4:
            ra, la = zb.at[w, zs(9 - s)], zb.at[w, zs(s - 1)]
        elif s == 4:
            ra, la = zb.at[w, zs(5), 0], zb.at[w, zs(3), 1]
        else:
            return
        ring[w] = [send(ra, ra, right), send(la, la, left)]

    def step(a, d):
        own_rows[a].done((d,))
        for k in range(2):
            total = None
            for j in range(4):
                px, py = (j, ys(d)) if k == 0 else (xs(d), j)
                lhs = jnp.concatenate([xc[a, k, h, px, py] for h in range(2)], axis=1)
                cols = wide(px * NY + py)
                part = dot(lhs, win[k, cols, :]) if a == 0 else dot(lhs, wout[k, :, cols], 1, 1)
                total = part if total is None else total + part
            acc[a, k] = total if d == 0 else acc[a, k] + total

    for sp in own_rows:
        sp.first()

    @pl.when(away)
    def _():
        cross.start()

    @pl.when(jnp.logical_not(away))
    def _():
        xd[:, c, x, y] = cross_out[...]

    for sp in own_rows:
        sp.second()
    loads[2].wait()
    loads[3].wait()
    step(0, 0)
    own_rows[0].forward()
    step(1, 0)
    own_rows[1].forward()

    step(0, 3)
    step(0, 1)
    own_rows[0].last()
    @pl.when(away)
    def _():
        cross.wait_recv()

    all_rows.first()
    step(1, 3)
    step(0, 2)
    own_rows[1].last()
    for k in range(2):
        hidden = acc[0, k]
        tang = jnp.tanh(GELU_SCALE * (hidden + GELU_CUBIC * hidden * hidden * hidden))
        slope = 0.5 * (1.0 + tang) + 0.5 * hidden * (1.0 - tang * tang) * GELU_SCALE * (
            1.0 + 3.0 * GELU_CUBIC * hidden * hidden
        )
        acc[0, k] = slope
        zb[0, r, k] = (0.5 * hidden * (1.0 + tang)).astype(BF)
    zstep(0, 1)
    step(1, 1)
    step(1, 2)
    for k in range(2):
        zb[1, r, k] = (gate_col[k][:, 0:1] * acc[1, k] * acc[0, k]).astype(BF)
    zstep(1, 1)
    pair, stage1, stage2, gates_on_way, kept = {}, {0: [], 1: []}, {0: [], 1: []}, {}, {}
    outs = []

    def leave(src, dst):
        cp = pltpu.make_async_copy(src, dst, osem.at[len(outs)])
        cp.start()
        outs.append(cp)

    def slot_part(k):
        pair[k] = []
        for n in range(2):

            @pl.loop(2 * n, 2 * n + 2)
            def _(i):
                for j in range(NY):
                    part = dot(win[k, wide(i * NY + j), :], zb[1, r, k], 1, 1).astype(BF)
                    for h in range(2):
                        ps[k, h, i, j] = part[h * COL : (h + 1) * COL]

            at = slice(2 * n, 2 * n + 2)
            pair[k].append(send(ps.at[k, oc, at], rsib.at[k, at], sib))

    def pair_sum(k):
        for n in range(2):
            pair[k][n].wait_recv()

            @pl.loop(2 * n, 2 * n + 2)
            def _(i):
                for j in range(NY):
                    ps[k, c, i, j] = (ps[k, c, i, j].astype(F32) + rsib[k, i, j].astype(F32)).astype(BF)

        for d in (1, 3, 2):
            if k == 0:
                stage1[k].append(send(ps.at[0, c, xs(d)], rs1.at[0, x], dev(r, xs(d), y, c)))
            else:
                stage1[k].append(send(ps.at[1, c, :, ys(d)], rs1.at[1, y], dev(r, x, ys(d), c)))

    def first_sum(k):
        for cp in stage1[k]:
            cp.wait_recv()
        for j in range(4):
            total = (ps[0, c, x, j] if k == 0 else ps[1, c, j, y]).astype(F32)
            for d in (1, 2, 3):
                total += rs1[k, xs(d) if k == 0 else ys(d), j].astype(F32)
            ts[k, j] = total.astype(BF)
        for d in (1, 3, 2):
            if k == 0:
                stage2[k].append(send(ts.at[0, ys(d)], rs2.at[0, y], dev(r, x, ys(d), c)))
            else:
                stage2[k].append(send(ts.at[1, xs(d)], rs2.at[1, x], dev(r, xs(d), y, c)))

    def return_rows():
        expand = jnp.concatenate([hot(pos_row[k] == iota((PAD, CAP), 0)) for k in range(2)], axis=1)
        sums = []
        for k in range(2):
            for cp in stage2[k]:
                cp.wait_recv()
            total = ts[k, y if k == 0 else x].astype(F32)
            for d in (1, 2, 3):
                total += rs2[k, ys(d) if k == 0 else xs(d)].astype(F32)
            sums.append(total.astype(BF))
        sums = jnp.concatenate(sums, axis=1)
        ob[...] = dot(expand, sums, 1, 1).astype(BF).reshape(2, NX, NY, ROWS, COL)
        kept["back"] = plane(ob, rb, bsem, brsem)
        rb[c, x, y] = ob[c, x, y]

    def gate_sum(n):
        if n == 0:
            for k in range(2):
                gbuf[0, k] = lax.dot_general(
                    jnp.ones((8, F), F32), zb[0, r, k].astype(F32) * acc[1, k], (((1,), (1,)), ((), ())),
                    precision=lax.Precision.HIGHEST, preferred_element_type=F32,
                )
            gates_on_way[0] = [send(gbuf.at[0], gsib, sib)]
            return
        for cp in gates_on_way[n - 1]:
            cp.wait_recv()
        if n == 1:
            gbuf[1] = gbuf[0] + gsib[...]
            gx[x] = gbuf[1]
            gates_on_way[1] = [send(gbuf.at[1], gx.at[x], dev(r, xs(d), y, c)) for d in (1, 3, 2)]
        elif n == 2:
            gbuf[2] = (gx[0] + gx[1]) + (gx[2] + gx[3])
            gy[y] = gbuf[2]
            gates_on_way[2] = [send(gbuf.at[2], gy.at[y], dev(r, x, ys(d), c)) for d in (1, 3, 2)]
        else:
            total = (gy[0] + gy[1]) + (gy[2] + gy[3])
            for k in range(2):
                dgate_ref[0, k : k + 1, :] = total[k, 0:1, :]
            leave(dgate_ref, dgate_hbm)

    def column_spread(n):
        (None, None, all_rows.second, all_rows.forward, all_rows.last)[n]()

    def owner_pick():
        unpick = jnp.zeros((TOK, ROWS), F32)
        for k in range(2):
            bt = hot(ch_row[k] - e * TOK == iota((TOK, CAP), 0))
            at = hot(pos_col[k] - my_first == iota((CAP, ROWS), 1))
            unpick += dot(bt, at)
        unpick_ref[...] = unpick.astype(BF)
        leave(unpick_ref, unpick_hbm)

    steps = {
        "slot": slot_part, "pair": pair_sum, "sum": first_sum, "back": return_rows, "gate": gate_sum,
        "ring": zstep, "cols": column_spread, "pick": owner_pick,
    }
    for name, *at in ORDER:
        steps[name](*at)

    def factor(w, k):
        return jnp.concatenate([zb[w, zs((NZ - g) % NZ), k] for g in range(NZ)], axis=0)

    def columns(a, k, j):
        blocks = [
            jnp.concatenate([xd[k, h, g // 2, 2 * (g % 2) + j, a] for g in range(NZ)], axis=0)
            for h in range(2)
        ]
        return jnp.concatenate(blocks, axis=1)

    zstep(0, 5)
    all_rows.done()
    for k in range(2):
        for j in range(2):
            at = slice(j * 2 * COL, (j + 1) * 2 * COL)
            dwout_ref[k, :, at] = dot(factor(0, k), columns(1, k, j), 0, 0).astype(BF)
    leave(dwout_ref, dwout_hbm)
    zstep(1, 5)
    for k in range(2):
        for j in range(2):
            at = slice(j * 2 * COL, (j + 1) * 2 * COL)
            dwin_ref[k, at, :] = dot(columns(0, k, j), factor(1, k), 0, 0).astype(BF)
    leave(dwin_ref, dwin_hbm)

    assert counter[0] <= NSEM, counter[0]
    for cp in sent + forth:
        cp.wait_send()

    @pl.when(away)
    def _():
        cross.wait_send()

    for cp in kept["back"]:
        cp.wait_recv()

    @pl.loop(0, NX)
    def _(i):
        for j in range(NY):
            to = turned(i * NY + j)
            rows_out[:, to // NY, lax.rem(to, NY)] = rb[:, i, j]

    leave(rows_out, rows_hbm)

    for cp in kept["back"]:
        cp.wait_send()
    for cp in outs:
        cp.wait()


def finish(
    rows_hbm, unpick_hbm, gate_hbm, win_hbm, wout_hbm, dtok_hbm, dgate_hbm, dwin_hbm, dwout_hbm,
    rows, unpick, gate, win, wout, dtok, isem, osem,
):
    ins = [
        pltpu.make_async_copy(src, dst, isem.at[i])
        for i, (src, dst) in enumerate(
            ((rows_hbm, rows), (unpick_hbm, unpick), (gate_hbm, gate), (win_hbm, win), (wout_hbm, wout))
        )
    ]
    for cp in ins:
        cp.start()
    outs = []

    def leave(src, dst):
        cp = pltpu.make_async_copy(src, dst, osem.at[len(outs)])
        cp.start()
        outs.append(cp)

    ins[0].wait()
    ins[1].wait()
    for i in range(NX):
        block = jnp.concatenate([rows[h, i, j] for j in range(NY) for h in range(2)], axis=1)
        at = pl.ds(i * BLK, BLK)
        dtok[0, :, at] = dot(unpick[...], block).astype(BF)
        leave(dtok.at[0, :, at], dtok_hbm.at[0, :, at])
    for cp, src, dst in zip(ins[2:], (gate, win, wout), (dgate_hbm, dwin_hbm, dwout_hbm)):
        cp.wait()
        leave(src, dst)
    for cp in outs:
        cp.wait()


def local(tokens, grad_out, gates, chosen, w_in, w_out):
    hbm = pl.BlockSpec(memory_space=pl.ANY)
    vmem = pl.BlockSpec(memory_space=pltpu.VMEM)
    dma = pltpu.SemaphoreType.DMA
    d_gate = jax.ShapeDtypeStruct((1, 2, CAP), F32)
    d_in = jax.ShapeDtypeStruct((2, D // NZ, F), BF)
    d_out = jax.ShapeDtypeStruct((2, F, D // NZ), BF)
    parts = pl.pallas_call(
        kernel,
        out_shape=(
            jax.ShapeDtypeStruct((2, NX, NY, ROWS, COL), BF),
            jax.ShapeDtypeStruct((TOK, ROWS), BF),
            d_gate,
            d_in,
            d_out,
        ),
        in_specs=[hbm, hbm, vmem, vmem, hbm, hbm],
        out_specs=(hbm,) * 5,
        scratch_shapes=[
            pltpu.VMEM((TOK, ROWS), BF),
            pltpu.VMEM((1, 2, CAP), F32),
            pltpu.VMEM((2, D // NZ, F), BF),
            pltpu.VMEM((2, F, D // NZ), BF),
            pltpu.VMEM((TOK, D), BF),
            pltpu.VMEM((TOK, D), BF),
            pltpu.VMEM((2, D, F), BF),
            pltpu.VMEM((2, F, D), BF),
            pltpu.VMEM((2, NX, NY, 2, ROWS, COL), BF),
            pltpu.VMEM((2, NX, NY, 2, ROWS, COL), BF),
            pltpu.VMEM((2, 2, 2, NX, NY, CAP, COL), BF),
            pltpu.VMEM((2, 2, CAP, COL), BF),
            pltpu.VMEM((2, 2, NX, NY, 2, CAP, COL), BF),
            pltpu.VMEM((2, NZ, 2, CAP, F), BF),
            pltpu.VMEM((2, 2, CAP, F), F32),
            pltpu.VMEM((2, 2, NX, NY, CAP, COL), BF),
            pltpu.VMEM((2, NX, NY, CAP, COL), BF),
            pltpu.VMEM((2, 4, 4, CAP, COL), BF),
            pltpu.VMEM((2, 4, CAP, COL), BF),
            pltpu.VMEM((2, 4, CAP, COL), BF),
            pltpu.VMEM((2, NX, NY, ROWS, COL), BF),
            pltpu.VMEM((2, NX, NY, ROWS, COL), BF),
            pltpu.VMEM((2, NX, NY, ROWS, COL), BF),
            pltpu.VMEM((3, 2, 8, CAP), F32),
            pltpu.VMEM((2, 8, CAP), F32),
            pltpu.VMEM((4, 2, 8, CAP), F32),
            pltpu.VMEM((4, 2, 8, CAP), F32),
            dma((NSEM,)),
            dma((NSEM,)),
            dma((PLANE,)),
            dma((PLANE,)),
            dma((PLANE,)),
            dma((PLANE,)),
            dma((4,)),
            dma((5,)),
            dma((2,)),
        ],
        compiler_params=pltpu.CompilerParams(
            collective_id=0, has_side_effects=True, vmem_limit_bytes=60 << 20
        ),
        name="expert_backward",
    )(tokens, grad_out, gates, chosen, w_in, w_out)
    return pl.pallas_call(
        finish,
        out_shape=(jax.ShapeDtypeStruct((1, TOK, D), BF), d_gate, d_in, d_out),
        in_specs=[hbm] * 5,
        out_specs=(hbm,) * 4,
        scratch_shapes=[
            pltpu.VMEM((2, NX, NY, ROWS, COL), BF),
            pltpu.VMEM((TOK, ROWS), BF),
            pltpu.VMEM((1, 2, CAP), F32),
            pltpu.VMEM((2, D // NZ, F), BF),
            pltpu.VMEM((2, F, D // NZ), BF),
            pltpu.VMEM((1, TOK, D), BF),
            dma((5,)),
            dma((7,)),
        ],
        compiler_params=pltpu.CompilerParams(vmem_limit_bytes=60 << 20),
        name="finish",
    )(*parts)


def solution(mesh):
    return jax.shard_map(
        local,
        mesh=mesh,
        in_specs=(
            P("rep", "exp", None),
            P("rep", "exp", None),
            P("rep", None, None),
            P("rep", None, None),
            P(None, None, "exp"),
            P(None, "exp", None),
        ),
        out_specs=(
            P("rep", "exp", None),
            P("rep", None, None),
            P(None, "rep", "exp"),
            P(None, "exp", "rep"),
        ),
        check_vma=False,
    )
```
